512 devices in a mesh: pipe: 128 (over y, z, x_lo), seq: 4 (over x_hi, core).
Axes of the slice: x: 4 (x_hi: 2, x_lo: 2; x = x_hi * 2 + x_lo), y: 4, z: 16, core: 2. Of those that a mesh axis runs over, the one named last changes fastest.
Arguments:
- activations: bfloat16 [32768, 3072], P(('pipe', 'seq')), may hold values from -200 to 200
- key_cache: bfloat16 [128, 1024, 1536], P('pipe', None, 'seq'), may hold values from -30 to 30
- value_cache: bfloat16 [128, 1024, 1536], P('pipe', None, 'seq'), may hold values from -6 to 6
- w_out: bfloat16 [128, 1536, 3072], P('pipe', 'seq'), may hold values from -0.15625 to 0.15625
- mod_shift: float32 [128, 3072], P('pipe'), may hold values from -3 to 3
- mod_scale: float32 [128, 3072], P('pipe'), may hold values from -2.5 to 2.5
- mod_gate: float32 [128, 3072], P('pipe'), may hold values from -12 to 12
- q_gain: float32 [128, 128], P('pipe'), may hold values from 0.5 to 6
- k_gain: float32 [128, 128], P('pipe'), may hold values from 0.5 to 6
- lengths: int32 [4], replicated, may hold values from 1 to 256, 960 in all
- first_patch: int32 [1], replicated, may hold values from 0 to 16383
Outputs:
- carried: bfloat16 [32768, 3072], P(('pipe', 'seq'))
The draws below stay inside these ranges and needn't reach their ends.
Inputs may be any that keep to these rules, and one draw needn't show every extreme that they name: `lengths`: in sequence order; they sum to 960 and the longest is exactly 256.
All inputs are finite; a program needn't handle non-finite values.
Results may differ from the reference program's by a relative error of at most 0.018.
Values may be sent and summed in bfloat16 or wider, within the bound.
A program may use at most 64 MiB of HBM per device.

```python
import math
import jax
import jax.numpy as jnp
import numpy as np
from jax import lax

D = 3072
HEADS = 12
HD = 128
NP = 4
TICKS = 2
ATT = 1536
PATCH = 256
SEQ_CAP = 1024
TOTAL = 960
N_PIPE = 128
N_SEQ = 4


def log_spread(key, lowest, highest):
    return jnp.exp(jax.random.uniform(key, (N_PIPE, HD), minval=math.log(lowest), maxval=math.log(highest)))


def draw_activations(key, part):
    key = jax.random.fold_in(key, 11)
    key_noise, key_spread = jax.random.split(key, 2)
    row_total = N_PIPE * PATCH
    column = jnp.arange(D, dtype=jnp.float32) / D
    spread = jax.random.uniform(key_spread, (D,), minval=0.0, maxval=1.0)
    col_scale = 3.0 ** column * 2.0 ** spread
    values = jnp.clip(jax.random.normal(key_noise, (row_total, D)), -4.0, 4.0) * col_scale
    return values.astype(jnp.bfloat16)


def draw_key_cache(key, part):
    key = jax.random.fold_in(key, 12)
    key_noise = jax.random.fold_in(key, 0)
    base_noise = jnp.clip(jax.random.normal(key_noise, (N_PIPE, SEQ_CAP, ATT)), -6.0, 6.0)
    values = base_noise
    return values.astype(jnp.bfloat16)


def draw_q_gain(key, part):
    key = jax.random.fold_in(key, 13)
    return log_spread(key, 0.5, 2.5)


def draw_k_gain(key, part):
    key = jax.random.fold_in(key, 14)
    return log_spread(key, 0.5, 2.5)


def steps_of(rng, dims, cuts, smallest, high):
    factor_of, own = 1.0, jax.random.fold_in(rng, 6)
    for dim, shards_of in cuts:
        draws = jnp.exp(jax.random.uniform(jax.random.fold_in(own, dim), (shards_of,), jnp.float32, smallest / len(cuts), high / len(cuts)))
        factor_of = factor_of * jnp.repeat(draws, dims[dim] // shards_of).reshape([-1 if axis == dim else 1 for axis in range(len(dims))])
    return factor_of


def profile(number_of, total, reach, slope):
    weights = [(1 << 20) // math.isqrt(grade ** slope) + 1 for grade in range(2, number_of + 1)]
    spare, counts = total - reach - (number_of - 1), [1] * (number_of - 1)
    while spare > 0:
        movable = [i for i in range(number_of - 1) if counts[i] < reach]
        mass, budget = sum([weights[i] for i in movable]), spare
        for i in movable:
            extra = min(reach - counts[i], max(1, budget * weights[i] // mass), spare)
            counts[i] = counts[i] + extra
            spare = spare - extra
    return np.array([reach] + counts)


def ragged(own_key, amount, total, reach, slope):
    if amount == 2:
        one = jax.random.randint(own_key, (), max(1, total - reach), min(reach, total - 1) + 1)
        return jnp.stack([one, total - one])
    tallies = jnp.asarray(profile(amount, total, reach, slope), jnp.int32)
    twos = (amount - 1) // 2
    source_of, receiver = tallies[1:1 + 2 * twos:2], tallies[2:2 + 2 * twos:2]
    room = jnp.minimum(source_of - 1, reach - receiver)
    shifted = jax.random.randint(jax.random.fold_in(own_key, 1), (twos,), 0, 1 << 20) % (room + 1)
    tallies = tallies.at[1:1 + 2 * twos:2].set(source_of - shifted).at[2:2 + 2 * twos:2].set(receiver + shifted)
    return tallies[jax.random.permutation(jax.random.fold_in(own_key, 2), amount)]


def scatter_about(stream_key, extent, scale, most, cuts=(), held_as=jnp.bfloat16):
    values = scale * jax.random.normal(stream_key, extent, jnp.float32)
    if cuts:
        values = values * steps_of(stream_key, extent, cuts, -0.22, 0.18)
    return jnp.clip(values, -most, most).astype(held_as)


def setup_inputs(seed: int = 0) -> dict:
    streams_of = jax.random.split(jax.random.key(seed), 12)
    return {
        "activations": draw_activations(jax.random.fold_in(streams_of[11], 71), 0),
        "key_cache": draw_key_cache(jax.random.fold_in(streams_of[11], 71), 0),
        "value_cache": scatter_about(streams_of[2], (N_PIPE, SEQ_CAP, ATT), 1.0, 6.0, ((0, 128), (2, 4))),
        "w_out": scatter_about(streams_of[3], (N_PIPE, ATT, D), ATT ** -0.5, 0.15625, ((0, 128), (1, 4))),
        "mod_shift": scatter_about(streams_of[4], (N_PIPE, D), 0.5, 3.0, ((0, 128),), jnp.float32),
        "mod_scale": scatter_about(streams_of[5], (N_PIPE, D), 0.4, 2.5, ((0, 128),), jnp.float32),
        "mod_gate": scatter_about(streams_of[6], (N_PIPE, D), 3.0, 12.0, ((0, 128),), jnp.float32),
        "q_gain": draw_q_gain(jax.random.fold_in(streams_of[11], 71), 0),
        "k_gain": draw_k_gain(jax.random.fold_in(streams_of[11], 71), 0),
        "lengths": ragged(streams_of[9], NP, TOTAL, PATCH, 0).astype(jnp.int32),
        "first_patch": jax.random.randint(streams_of[10], (1,), 0, NP * 4096).astype(jnp.int32),
    }


epsilon = 1e-06
masked_score = -1e+30

def refresh(stored, fresh_rows, first_row, length):
    total_rows = stored.shape[0]
    padded = jnp.zeros((total_rows + fresh_rows.shape[0], stored.shape[1]), stored.dtype)
    placed = lax.dynamic_update_slice(padded, fresh_rows, (first_row.astype(jnp.int32), jnp.int32(0)))[:total_rows]
    row_index = jnp.arange(total_rows, dtype=jnp.int32)
    inside = (row_index >= first_row) & (row_index < first_row + length)
    return jnp.where(inside[:, None], placed, stored)

def modulate(values, shift_row, scale_row):
    row_mean = lax.optimization_barrier(jnp.mean(values, axis=1, keepdims=True))
    centred = values - row_mean
    variance = lax.optimization_barrier(jnp.mean(centred * centred, axis=1, keepdims=True))
    return (centred / jnp.sqrt(variance + epsilon) * (1.0 + scale_row) + shift_row).astype(jnp.bfloat16)

def head_parts(head_input, query_gain, key_gain):
    head_values = head_input.astype(jnp.float32).reshape(head_input.shape[0], -1, HD)
    head_rms = jnp.sqrt(lax.optimization_barrier(jnp.mean(head_values * head_values, axis=2, keepdims=True)) + epsilon)
    normed = head_values / head_rms
    queries = (normed * query_gain).astype(jnp.bfloat16)
    fresh_keys = (normed * key_gain).astype(jnp.bfloat16).reshape(head_input.shape)
    return (queries, fresh_keys)

def section_step(carried, key_store, value_store, out_weight, shift_row, scale_row, gate_row, query_gain, key_gain, first_row, length):
    values = carried.astype(jnp.float32)
    modded = modulate(values, shift_row, scale_row)
    head_input = modded[:, :ATT]
    queries, fresh_keys = head_parts(head_input, query_gain, key_gain)
    key_store = refresh(key_store, fresh_keys, first_row, length)
    value_store = refresh(value_store, head_input, first_row, length)
    key_rows = key_store.astype(jnp.float32).reshape(SEQ_CAP, HEADS, HD)
    value_rows = value_store.astype(jnp.float32).reshape(SEQ_CAP, HEADS, HD)
    scores = jnp.einsum('qhd,khd->hqk', queries.astype(jnp.float32), key_rows) * HD ** (-0.5)
    live_keys = jnp.arange(SEQ_CAP, dtype=jnp.int32) < TOTAL
    scores = jnp.where(live_keys[None, None, :], scores, masked_score)
    row_max = lax.optimization_barrier(jnp.max(scores, axis=2, keepdims=True))
    weight = jnp.exp(scores - row_max)
    probability = (weight / lax.optimization_barrier(jnp.sum(weight, axis=2, keepdims=True))).astype(jnp.bfloat16)
    attended = jnp.einsum('hqk,khd->qhd', probability.astype(jnp.float32), value_rows)
    attended = attended.astype(jnp.bfloat16).reshape(PATCH, N_SEQ, ATT // N_SEQ)
    grouped_weight = out_weight.astype(jnp.float32).reshape(N_SEQ, ATT // N_SEQ, D)
    partial_value = jnp.einsum('qgc,gcd->gqd', attended.astype(jnp.float32), grouped_weight).astype(jnp.bfloat16)
    partial_value = lax.optimization_barrier(partial_value)
    projected = lax.optimization_barrier(jnp.sum(partial_value.astype(jnp.float32), axis=0))
    updated = values + gate_row * projected
    live_rows = jnp.arange(PATCH, dtype=jnp.int32) < length
    updated = jnp.where(live_rows[:, None], updated, 0.0).astype(jnp.bfloat16)
    return (updated, key_store, value_store)

def reference(activations, key_cache, value_cache, w_out, mod_shift, mod_scale, mod_gate, q_gain, k_gain, lengths, first_patch):
    patch_lengths = lengths.astype(jnp.int32)
    first_rows = (jnp.cumsum(patch_lengths) - patch_lengths).astype(jnp.int32)
    carried = activations.reshape(N_PIPE, PATCH, D)
    key_store = key_cache
    value_store = value_cache
    sections = jnp.arange(N_PIPE, dtype=jnp.int32)
    for segment_step in range(TICKS):

        def advance(pieces):
            section = pieces[-1]
            patch_id = (first_patch[0] + segment_step - section) % NP
            updated, new_keys, new_values = section_step(pieces[0], pieces[1], pieces[2], pieces[3], pieces[4], pieces[5], pieces[6], pieces[7], pieces[8], first_rows[patch_id], patch_lengths[patch_id])
            return (updated, new_keys, new_values)
        carried, key_store, value_store = lax.map(advance, (carried, key_store, value_store, w_out, mod_shift, mod_scale, mod_gate, q_gain, k_gain, sections))
        carried = jnp.roll(carried, 1, axis=0)
    return carried.reshape(N_PIPE * PATCH, D)
```

```python
import functools
import math

import jax
import jax.numpy as jnp
from jax import lax
from jax.experimental import pallas as pl
from jax.experimental.pallas import tpu as pltpu
from jax.sharding import PartitionSpec as P

MESH = pl.DeviceIdType.MESH
BF16 = jnp.bfloat16
F32 = jnp.float32

NP = 4
EPS = 1e-06
MASKED = -1e30
HD = 128
BLK = 384
SLAB = 2 * BLK
ROWS = 64
PATCH = 256
CAP = 1024
TOTAL = 960
WIDTH = 3072
HALF = WIDTH // 2
EXP2_SCALE = math.log2(math.e) / math.sqrt(HD)


def mult(value, of):
    return pl.multiple_of(value, of)


def kernel(
    n_pipe,
    x_hbm,
    k_hbm,
    v_hbm,
    w_hbm,
    shift_hbm,
    scale_hbm,
    gate_hbm,
    qg_hbm,
    kg_hbm,
    lengths,
    first_patch,
    out_hbm,
    xv,
    kv,
    vv,
    w4,
    shv,
    scv,
    gav,
    qgv,
    kgv,
    xh,
    st1,
    res,
    qb,
    fh,
    att1,
    sb1,
    rb,
    xs,
    st2,
    rx,
    as2,
    att2,
    sb2,
    lsem,
    xh_s,
    xh_r,
    st_s,
    st_r,
    res_s,
    res_r,
    w_s,
    w_r,
    a1_s,
    a1_r,
    p1_s,
    p1_r,
    s2_s,
    s2_r,
    rx_s,
    rx_r,
    a2_s,
    a2_r,
    p2_s,
    p2_r,
):
    s = lax.axis_index("pipe")
    q = lax.axis_index("seq")
    j = q // 2
    c = q % 2
    nxt = (s + 1) % n_pipe
    prv = (s + n_pipe - 1) % n_pipe
    chip = [j, 1 - j]
    slab = [2 * chip[0] + c, 2 * chip[1] + c]
    mate_slab = [2 * chip[0] + (1 - c), 2 * chip[1] + (1 - c)]
    peer = {1: mate_slab[0], 2: slab[1], 3: mate_slab[1]}
    mate = peer[1]

    def remote(src, dst, ssem, rsem, pipe, seq):
        return pltpu.make_async_remote_copy(
            src_ref=src,
            dst_ref=dst,
            send_sem=ssem,
            recv_sem=rsem,
            device_id={"pipe": pipe, "seq": seq},
            device_id_type=MESH,
        )

    local = []

    def load(src, dst):
        copy = pltpu.make_async_copy(src, dst, lsem.at[len(local)])
        copy.start()
        local.append(copy)
        return copy

    ld_x = load(x_hbm, xv)
    ld_small = [
        load(shift_hbm, shv),
        load(scale_hbm, scv),
        load(gate_hbm, gav),
        load(qg_hbm, qgv),
        load(kg_hbm, kgv),
    ]
    ld_xh = load(x_hbm.at[:, pl.ds(mult(BLK * q, 128), BLK)], xh.at[pl.ds(mult(ROWS * q, ROWS), ROWS)])
    ld_k = load(k_hbm.at[0], kv)
    ld_v = load(v_hbm.at[0], vv)

    bar = pltpu.get_barrier_semaphore()
    for k in (1, 2, 3):
        pl.semaphore_signal(bar, inc=1, device_id={"pipe": s, "seq": peer[k]}, device_id_type=MESH)
    for v in (0, 1):
        pl.semaphore_signal(bar, inc=1, device_id={"pipe": prv, "seq": slab[v]}, device_id_type=MESH)
    pl.semaphore_wait(bar, 5)

    xh_copies = {}
    for k in (2, 3, 1):
        xh_copies[k] = remote(
            x_hbm.at[:, pl.ds(mult(BLK * peer[k], 128), BLK)],
            xh.at[pl.ds(mult(ROWS * q, ROWS), ROWS)],
            xh_s.at[k - 1],
            xh_r.at[k - 1],
            s,
            peer[k],
        )
        xh_copies[k].start()

    ld_res = []
    res_copies = []
    for v in (0, 1):
        for e in (0, 1):
            dst = res.at[v, pl.ds(mult(ROWS * c, ROWS), ROWS), pl.ds(BLK * e, BLK)]
            ld_res.append(load(x_hbm.at[:, pl.ds(mult(HALF * e + BLK * slab[v], 128), BLK)], dst))
            copy = remote(
                x_hbm.at[:, pl.ds(mult(HALF * e + BLK * mate_slab[v], 128), BLK)],
                dst,
                res_s.at[2 * v + e],
                res_r.at[2 * v + e],
                s,
                mate,
            )
            copy.start()
            res_copies.append(copy)

    ld_w = []
    w_copies = []
    for n, (mine, his) in enumerate(
        [(slab[0], mate_slab[0]), (slab[1], mate_slab[1]), (mate_slab[0], slab[0]), (mate_slab[1], slab[1])]
    ):
        for e in (0, 1):
            for g, away in ((mine, False), (his, True)):
                src = w_hbm.at[0, :, pl.ds(mult(HALF * e + BLK * g, 128), BLK)]
                dst = w4.at[g, pl.ds(mult(BLK * c, BLK), BLK), pl.ds(BLK * e, BLK)]
                if away:
                    copy = remote(src, dst, w_s.at[2 * n + e], w_r.at[2 * n + e], s, mate)
                    copy.start()
                    w_copies.append(copy)
                else:
                    ld_w.append(load(src, dst))

    ld_x.wait()
    xf = xv[...].astype(F32)
    mean = jnp.sum(xf, axis=1, keepdims=True) * (1.0 / WIDTH)
    cent = xf - mean
    var = jnp.sum(cent * cent, axis=1, keepdims=True) * (1.0 / WIDTH)
    rstd = lax.rsqrt(var + EPS)
    lane = lax.broadcasted_iota(jnp.int32, (ROWS, 128), 1)
    st1[pl.ds(mult(ROWS * q, ROWS), ROWS), :] = jnp.where(lane == 0, mean, rstd)
    st_copies = {}
    for k in (2, 3, 1):
        part = st1.at[pl.ds(mult(ROWS * q, ROWS), ROWS)]
        st_copies[k] = remote(part, part, st_s.at[k - 1], st_r.at[k - 1], s, peer[k])
        st_copies[k].start()

    for copy in ld_small:
        copy.wait()
    scale_h = 1.0 + scv[:, pl.ds(mult(BLK * q, 128), BLK)]
    shift_h = shv[:, pl.ds(mult(BLK * q, 128), BLK)]
    q_gain = qgv[...]
    k_gain = kgv[...]

    def patch_at(t):
        p = (first_patch[0] + t + n_pipe * NP - s) % NP
        first = jnp.int32(0)
        length = jnp.int32(0)
        for n in range(NP):
            first = first + jnp.where(n < p, lengths[n], 0)
            length = length + jnp.where(n == p, lengths[n], 0)
        return first, length

    def prep_rows(raw, mean, rstd, rows):
        modded = ((raw - mean) * rstd * scale_h + shift_h).astype(BF16)
        fh[rows, BLK:] = modded
        mf = modded.astype(F32)
        for h in range(BLK // HD):
            part = mf[:, HD * h : HD * (h + 1)]
            rms = jnp.sqrt(jnp.mean(part * part, axis=1, keepdims=True) + EPS)
            normed = part / rms
            qb[rows, HD * h : HD * (h + 1)] = (normed * q_gain).astype(BF16)
            fh[rows, HD * h : HD * (h + 1)] = (normed * k_gain).astype(BF16)

    def refresh(first, length):
        def block(n, carry):
            rows = pl.ds(mult(n * PATCH, PATCH), PATCH)
            row = lax.broadcasted_iota(jnp.int32, (PATCH, PATCH), 0) + n * PATCH
            col = lax.broadcasted_iota(jnp.int32, (PATCH, PATCH), 1)
            pick = jnp.where((row - first == col) & (col < length), 1.0, 0.0).astype(BF16)
            placed = jnp.dot(pick, fh[...], preferred_element_type=F32)
            at = lax.broadcasted_iota(jnp.int32, (PATCH, BLK), 0) + n * PATCH
            inside = (at >= first) & (at < first + length)
            kv[rows, :] = jnp.where(inside, placed[:, :BLK], kv[rows, :].astype(F32)).astype(BF16)
            vv[rows, :] = jnp.where(inside, placed[:, BLK:], vv[rows, :].astype(F32)).astype(BF16)
            return carry

        lax.fori_loop(0, CAP // PATCH, block, 0)

    def attend(queries, live):
        parts = []
        for h in range(BLK // HD):
            cols = slice(HD * h, HD * (h + 1))
            scores = lax.dot_general(
                queries[:, cols], kv[:, cols], (((1,), (1,)), ((), ())), preferred_element_type=F32
            )
            rows = scores.shape[0]
            tail = CAP - 128
            at = lax.broadcasted_iota(jnp.int32, (rows, 128), 1) + tail
            scores = jnp.concatenate(
                [scores[:, :tail], jnp.where(at < TOTAL, scores[:, tail:], MASKED)], axis=1
            )
            top = jnp.max(scores, axis=1, keepdims=True)
            weight = jnp.exp2((scores - top) * EXP2_SCALE)
            total = jnp.sum(weight, axis=1, keepdims=True)
            out = jnp.dot(weight.astype(BF16), vv[:, cols], preferred_element_type=F32)
            parts.append(jnp.where(live, out / total, 0.0).astype(BF16))
        return jnp.concatenate(parts, axis=1)

    def gates(g):
        lo = gav[:, pl.ds(mult(BLK * g, 128), BLK)]
        hi = gav[:, pl.ds(mult(HALF + BLK * g, 128), BLK)]
        return jnp.concatenate([lo, hi], axis=1)

    own_cols = pl.ds(mult(BLK * c, BLK), BLK)

    first, length = patch_at(0)
    for k in (1, 2, 3):
        xh_copies[k].wait_recv()
    ld_xh.wait()
    for k in (1, 2, 3):
        st_copies[k].wait_recv()

    def prep0(n, carry):
        rows = pl.ds(mult(n * ROWS, ROWS), ROWS)
        stat = st1[rows, :]
        prep_rows(xh[rows, :].astype(F32), stat[:, 0:1], stat[:, 1:2], rows)
        return carry

    lax.fori_loop(0, PATCH // ROWS, prep0, 0)
    ld_k.wait()
    ld_v.wait()
    refresh(first, length)

    def att1_copy(i):
        part = att1.at[pl.ds(mult(i * ROWS, ROWS), ROWS), own_cols]
        return remote(part, part, a1_s.at[i], a1_r.at[i], s, mate)

    def p1_copy(i, v):
        rows = pl.ds(mult(i * ROWS, ROWS), ROWS)
        return remote(sb1.at[v, rows], rb.at[v, rows], p1_s.at[v, i], p1_r.at[v, i], nxt, slab[v])

    for copy in ld_res:
        copy.wait()
    for copy in res_copies:
        copy.wait_recv()
    for copy in ld_w[:4]:
        copy.wait()
    for copy in w_copies[:4]:
        copy.wait_recv()

    gate1 = [gates(slab[0]), gates(slab[1])]

    def step0(i, carry):
        @pl.when(i < PATCH // ROWS)
        def _():
            rows = pl.ds(mult(i * ROWS, ROWS), ROWS)
            live = lax.broadcasted_iota(jnp.int32, (ROWS, HD), 0) + i * ROWS < length
            att1[rows, own_cols] = attend(qb[rows, :], live)
            att1_copy(i).start()

        @pl.when(i > 0)
        def _():
            n = i - 1
            att1_copy(n).wait_recv()
            rows = pl.ds(mult(n * ROWS, ROWS), ROWS)
            live = lax.broadcasted_iota(jnp.int32, (ROWS, SLAB), 0) + n * ROWS < length
            keep = live & (n // 2 == j)
            for v in (0, 1):
                proj = jnp.dot(att1[rows, :], w4[slab[v]], preferred_element_type=F32)
                held = res[v, pl.ds(mult((n % 2) * ROWS, ROWS), ROWS), :].astype(F32)
                sb1[v, rows, :] = (proj * gate1[v] + jnp.where(keep, held, 0.0)).astype(BF16)
                p1_copy(n, v).start()

        return carry

    lax.fori_loop(0, PATCH // ROWS + 1, step0, 0)

    st2[0] = jnp.zeros((ROWS, 128), F32)

    def take(i, carry):
        rows = pl.ds(mult(i * ROWS, ROWS), ROWS)
        for v in (0, 1):
            p1_copy(i, v).wait_recv()
        held = (rb[0, rows, :].astype(F32) + rb[1, rows, :].astype(F32)).astype(BF16)
        xs[rows, :] = held
        hf = held.astype(F32)
        mean = jnp.sum(hf, axis=1, keepdims=True) * (1.0 / SLAB)
        cent = hf - mean
        spread = jnp.sum(cent * cent, axis=1, keepdims=True)
        st2[0] = jnp.where(lane == 2 * i, mean, jnp.where(lane == 2 * i + 1, spread, st2[0]))
        return carry

    lax.fori_loop(0, PATCH // ROWS, take, 0)
    s2_copies = {}
    for k in (2, 3, 1):
        s2_copies[k] = remote(st2.at[0], st2.at[k], s2_s.at[k - 1], s2_r.at[k - 1], s, peer[k])
        s2_copies[k].start()
    rx_copies = []
    for v in (0, 1):
        src = xs.at[pl.ds(mult(ROWS * mate_slab[v], ROWS), ROWS)]
        copy = remote(src, rx.at[v], rx_s.at[v], rx_r.at[v], s, mate)
        copy.start()
        rx_copies.append(copy)

    first, length = patch_at(1)
    for k in (1, 2, 3):
        s2_copies[k].wait_recv()
    stats = [st2[k] for k in range(4)]
    for i in range(PATCH // ROWS):
        means = [stat[:, 2 * i : 2 * i + 1] for stat in stats]
        spreads = [stat[:, 2 * i + 1 : 2 * i + 2] for stat in stats]
        mean = (means[0] + means[1] + means[2] + means[3]) * 0.25
        spread = spreads[0] + spreads[1] + spreads[2] + spreads[3]
        for m in means:
            spread = spread + (m - mean) * (m - mean) * SLAB
        rstd = lax.rsqrt(spread * (1.0 / WIDTH) + EPS)
        rows = slice(i * ROWS, (i + 1) * ROWS)
        prep_rows(xs[rows, :BLK].astype(F32), mean, rstd, rows)

    refresh(first, length)

    half = ROWS // 2

    def att2_copy(i):
        rows = pl.ds(mult(i * ROWS, ROWS), ROWS)
        return remote(as2.at[rows], att2.at[rows, own_cols], a2_s.at[i], a2_r.at[i], s, mate)

    def p2_copy(i, v):
        rows = pl.ds(mult(i * half, half), half)
        return remote(sb2.at[v, rows], out_hbm.at[v, rows], p2_s.at[v, i], p2_r.at[v, i], nxt, slab[v])

    for copy in rx_copies:
        copy.wait_recv()
    for copy in ld_w[4:]:
        copy.wait()
    for copy in w_copies[4:]:
        copy.wait_recv()

    bases = [ROWS * slab[0], ROWS * slab[1], ROWS * mate_slab[0], ROWS * mate_slab[1]]
    order = [slab[0], mate_slab[0], slab[1], mate_slab[1]]

    def step1(i, carry):
        @pl.when(i < 2)
        def _():
            queries = jnp.concatenate(
                [qb[pl.ds(mult(base + half * i, half), half), :] for base in bases], axis=0
            )
            r = lax.broadcasted_iota(jnp.int32, (4 * half, HD), 0)
            seg = r // half
            base = jnp.where(
                seg == 0, bases[0], jnp.where(seg == 1, bases[1], jnp.where(seg == 2, bases[2], bases[3]))
            )
            live = base + half * i + r % half < length
            got = attend(queries, live)
            rows = pl.ds(mult(i * ROWS, ROWS), ROWS)
            att2[rows, own_cols] = got[:ROWS]
            as2[rows, :] = got[ROWS:]
            att2_copy(i).start()

        @pl.when(i > 0)
        def _():
            n = i - 1
            att2_copy(n).wait_recv()
            rows = pl.ds(mult(n * ROWS, ROWS), ROWS)
            part = pl.ds(mult(n * half, half), half)
            left = att2[rows, :]
            for at, g in enumerate(order):
                proj = jnp.dot(left, w4[g], preferred_element_type=F32) * gates(g)
                if at == 0:
                    proj = proj + jnp.concatenate(
                        [xs[pl.ds(mult(base + half * n, half), half), :] for base in bases[:2]], axis=0
                    ).astype(F32)
                if at == 1:
                    proj = proj + jnp.concatenate([rx[0, part, :], rx[1, part, :]], axis=0).astype(F32)
                proj = proj.astype(BF16)
                for v in (0, 1):
                    for e in (0, 1):
                        sb2[v, part, pl.ds(mult(HALF * e + BLK * g, 128), BLK)] = proj[
                            v * half : (v + 1) * half, e * BLK : (e + 1) * BLK
                        ]
            for v in (0, 1):
                p2_copy(n, v).start()

        return carry

    lax.fori_loop(0, 3, step1, 0)

    for k in (1, 2, 3):
        xh_copies[k].wait_send()
        st_copies[k].wait_send()
        s2_copies[k].wait_send()
    for copy in res_copies + w_copies + rx_copies:
        copy.wait_send()
    for i in range(PATCH // ROWS):
        att1_copy(i).wait_send()
        for v in (0, 1):
            p1_copy(i, v).wait_send()
    for i in range(2):
        att2_copy(i).wait_send()
        for v in (0, 1):
            p2_copy(i, v).wait()


def shards(n_pipe, *args):
    dma = pltpu.SemaphoreType.DMA
    any_space = pl.BlockSpec(memory_space=pl.ANY)
    hbm = pl.BlockSpec(memory_space=pltpu.HBM)
    smem = pl.BlockSpec(memory_space=pltpu.SMEM)
    chunks = PATCH // ROWS
    parts = pl.pallas_call(
        functools.partial(kernel, n_pipe),
        out_shape=jax.ShapeDtypeStruct((2, ROWS, WIDTH), BF16),
        in_specs=[hbm] * 9 + [smem] * 2,
        out_specs=any_space,
        scratch_shapes=[
            pltpu.VMEM((ROWS, WIDTH), BF16),
            pltpu.VMEM((CAP, BLK), BF16),
            pltpu.VMEM((CAP, BLK), BF16),
            pltpu.VMEM((4, SLAB, SLAB), BF16),
            pltpu.VMEM((1, WIDTH), F32),
            pltpu.VMEM((1, WIDTH), F32),
            pltpu.VMEM((1, WIDTH), F32),
            pltpu.VMEM((1, HD), F32),
            pltpu.VMEM((1, HD), F32),
            pltpu.VMEM((PATCH, BLK), BF16),
            pltpu.VMEM((PATCH, 128), F32),
            pltpu.VMEM((2, 2 * ROWS, SLAB), BF16),
            pltpu.VMEM((PATCH, BLK), BF16),
            pltpu.VMEM((PATCH, SLAB), BF16),
            pltpu.VMEM((PATCH, SLAB), BF16),
            pltpu.VMEM((2, PATCH, SLAB), BF16),
            pltpu.VMEM((2, PATCH, SLAB), BF16),
            pltpu.VMEM((PATCH, SLAB), BF16),
            pltpu.VMEM((4, ROWS, 128), F32),
            pltpu.VMEM((2, ROWS, SLAB), BF16),
            pltpu.VMEM((2 * ROWS, BLK), BF16),
            pltpu.VMEM((2 * ROWS, SLAB), BF16),
            pltpu.VMEM((2, ROWS, WIDTH), BF16),
            dma((24,)),
            dma((3,)),
            dma((3,)),
            dma((3,)),
            dma((3,)),
            dma((4,)),
            dma((4,)),
            dma((8,)),
            dma((8,)),
            dma((chunks,)),
            dma((chunks,)),
            dma((2, chunks)),
            dma((2, chunks)),
            dma((3,)),
            dma((3,)),
            dma((2,)),
            dma((2,)),
            dma((2,)),
            dma((2,)),
            dma((2, 2)),
            dma((2, 2)),
        ],
        compiler_params=pltpu.CompilerParams(
            collective_id=0, has_side_effects=True, vmem_limit_bytes=40 << 20
        ),
        name="section_steps",
    )(*args)
    return (parts[0].astype(F32) + parts[1].astype(F32)).astype(BF16)


def solution(mesh):
    in_specs = (
        P(("pipe", "seq"), None),
        P("pipe", None, "seq"),
        P("pipe", None, "seq"),
        P("pipe", "seq", None),
        P("pipe", None),
        P("pipe", None),
        P("pipe", None),
        P("pipe", None),
        P("pipe", None),
        P(),
        P(),
    )
    return jax.shard_map(
        functools.partial(shards, mesh.shape["pipe"]),
        mesh=mesh,
        in_specs=in_specs,
        out_specs=P(("pipe", "seq"), None),
        check_vma=False,
    )
```

```python
import functools
import math

import jax
import jax.numpy as jnp
from jax import lax
from jax.experimental import pallas as pl
from jax.experimental.pallas import tpu as pltpu
from jax.sharding import PartitionSpec as P

MESH = pl.DeviceIdType.MESH
BF16 = jnp.bfloat16
F32 = jnp.float32

NP = 4
EPS = 1e-06
MASKED = -1e30
HD = 128
BLK = 384
SLAB = 2 * BLK
ROWS = 64
PATCH = 256
CAP = 1024
UNIT = 32
UNITS = PATCH // UNIT
LAG = 2
TOTAL = 960
WIDTH = 3072
HALF = WIDTH // 2
EXP2_SCALE = math.log2(math.e) / math.sqrt(HD)


def mult(value, of):
    return pl.multiple_of(value, of)


def kernel(
    n_pipe,
    x_hbm,
    k_hbm,
    v_hbm,
    w_hbm,
    shift_hbm,
    scale_hbm,
    gate_hbm,
    qg_hbm,
    kg_hbm,
    lengths,
    first_patch,
    out_ref,
    xv,
    kv,
    vv,
    w4,
    shv,
    scv,
    gav,
    qgv,
    kgv,
    md,
    res,
    qb,
    fh,
    att1,
    sb1,
    rb1,
    fw1,
    xs,
    st2,
    rx,
    as2,
    att2,
    sb2,
    rb2,
    fw2,
    lsem,
    md_s,
    md_r,
    res_s,
    res_r,
    w_s,
    w_r,
    a1_s,
    a1_r,
    p1_s,
    p1_r,
    f1_s,
    f1_r,
    s2_s,
    s2_r,
    rx_s,
    rx_r,
    a2_s,
    a2_r,
    p2_s,
    p2_r,
    f2_s,
    f2_r,
):
    s = lax.axis_index("pipe")
    q = lax.axis_index("seq")
    j = q // 2
    c = q % 2
    odd = s % 2
    even = odd == 0
    pair = s + 1 - 2 * odd
    ahead = (s + 2) % n_pipe
    behind = (s + n_pipe - 2) % n_pipe
    chip = [j, 1 - j]
    slab = [2 * chip[0] + c, 2 * chip[1] + c]
    mate_slab = [2 * chip[0] + (1 - c), 2 * chip[1] + (1 - c)]
    peer = {1: mate_slab[0], 2: slab[1], 3: mate_slab[1]}
    mate = peer[1]
    own_rows = pl.ds(mult(ROWS * q, ROWS), ROWS)
    own_cols = pl.ds(mult(BLK * c, BLK), BLK)

    def block_cols(g, e):
        return pl.ds(mult(HALF * e + BLK * g, 128), BLK)

    def remote(src, dst, ssem, rsem, pipe, seq):
        return pltpu.make_async_remote_copy(
            src_ref=src,
            dst_ref=dst,
            send_sem=ssem,
            recv_sem=rsem,
            device_id={"pipe": pipe, "seq": seq},
            device_id_type=MESH,
        )

    bar = pltpu.get_barrier_semaphore()
    for k in (1, 2, 3):
        pl.semaphore_signal(bar, inc=1, device_id={"pipe": s, "seq": peer[k]}, device_id_type=MESH)
    for v in (0, 1):
        pl.semaphore_signal(bar, inc=1, device_id={"pipe": pair, "seq": slab[v]}, device_id_type=MESH)
    pl.semaphore_signal(bar, inc=1, device_id={"pipe": behind, "seq": q}, device_id_type=MESH)

    local = []

    def load(src, dst):
        copy = pltpu.make_async_copy(src, dst, lsem.at[len(local)])
        copy.start()
        local.append(copy)
        return copy

    ld_x = load(x_hbm, xv)
    ld_sc = load(scale_hbm, scv)
    ld_sh = load(shift_hbm, shv)
    ld_small = [load(gate_hbm, gav), load(qg_hbm, qgv), load(kg_hbm, kgv)]
    ld_k = load(k_hbm.at[0], kv)
    ld_v = load(v_hbm.at[0], vv)

    ld_x.wait()
    xf = xv[...].astype(F32)
    mean = jnp.sum(xf, axis=1, keepdims=True) * (1.0 / WIDTH)
    cent = xf - mean
    var = jnp.sum(cent * cent, axis=1, keepdims=True) * (1.0 / WIDTH)
    rstd = lax.rsqrt(var + EPS)
    ld_sc.wait()
    ld_sh.wait()
    md[...] = (
        (xv[:, :HALF].astype(F32) - mean) * rstd * (1.0 + scv[:, :HALF]) + shv[:, :HALF]
    ).astype(BF16)
    fh[own_rows, BLK:] = md[:, pl.ds(mult(BLK * q, 128), BLK)]

    pl.semaphore_wait(bar, 6)

    md_copies = {}
    for k in (2, 3, 1):
        md_copies[k] = remote(
            md.at[:, pl.ds(mult(BLK * peer[k], 128), BLK)],
            fh.at[own_rows, pl.ds(BLK, BLK)],
            md_s.at[k - 1],
            md_r.at[k - 1],
            s,
            peer[k],
        )
        md_copies[k].start()

    ld_res = []
    res_copies = []
    for v in (0, 1):
        for e in (0, 1):
            dst = res.at[v, pl.ds(mult(ROWS * c, ROWS), ROWS), pl.ds(BLK * e, BLK)]
            ld_res.append(load(x_hbm.at[:, block_cols(slab[v], e)], dst))
            copy = remote(
                x_hbm.at[:, block_cols(mate_slab[v], e)], dst, res_s.at[2 * v + e], res_r.at[2 * v + e], s, mate
            )
            copy.start()
            res_copies.append(copy)

    ld_w = []
    w_copies = []
    for n, (mine, his) in enumerate(
        [(slab[0], mate_slab[0]), (slab[1], mate_slab[1]), (mate_slab[0], slab[0]), (mate_slab[1], slab[1])]
    ):
        for e in (0, 1):
            for g, away in ((mine, False), (his, True)):
                src = w_hbm.at[0, :, block_cols(g, e)]
                dst = w4.at[g, own_cols, pl.ds(BLK * e, BLK)]
                if away:
                    copy = remote(src, dst, w_s.at[2 * n + e], w_r.at[2 * n + e], s, mate)
                    copy.start()
                    w_copies.append(copy)
                else:
                    ld_w.append(load(src, dst))

    for copy in ld_small:
        copy.wait()
    head_cols = pl.ds(mult(BLK * q, 128), BLK)
    scale_h = 1.0 + scv[:, head_cols]
    shift_h = shv[:, head_cols]
    q_gain = qgv[...]
    k_gain = kgv[...]

    def patch_at(t):
        p = (first_patch[0] + t + n_pipe * NP - s) % NP
        first = jnp.int32(0)
        length = jnp.int32(0)
        for n in range(NP):
            first = first + jnp.where(n < p, lengths[n], 0)
            length = length + jnp.where(n == p, lengths[n], 0)
        return first, length

    def heads(modded, rows):
        mf = modded.astype(F32)
        for h in range(BLK // HD):
            part = mf[:, HD * h : HD * (h + 1)]
            normed = part * lax.rsqrt(jnp.sum(part * part, axis=1, keepdims=True) * (1.0 / HD) + EPS)
            qb[rows, HD * h : HD * (h + 1)] = (normed * q_gain).astype(BF16)
            fh[rows, HD * h : HD * (h + 1)] = (normed * k_gain).astype(BF16)

    def refresh(first, length):
        def block(n, carry):
            rows = pl.ds(mult(n * PATCH, PATCH), PATCH)
            row = lax.broadcasted_iota(jnp.int32, (PATCH, PATCH), 0) + n * PATCH
            col = lax.broadcasted_iota(jnp.int32, (PATCH, PATCH), 1)
            pick = jnp.where((row - first == col) & (col < length), 1.0, 0.0).astype(BF16)
            placed = jnp.dot(pick, fh[...], preferred_element_type=F32)
            at = lax.broadcasted_iota(jnp.int32, (PATCH, BLK), 0) + n * PATCH
            inside = (at >= first) & (at < first + length)
            kv[rows, :] = jnp.where(inside, placed[:, :BLK], kv[rows, :].astype(F32)).astype(BF16)
            vv[rows, :] = jnp.where(inside, placed[:, BLK:], vv[rows, :].astype(F32)).astype(BF16)
            return carry

        lax.fori_loop(0, CAP // PATCH, block, 0)

    def attend(queries, live):
        parts = []
        for h in range(BLK // HD):
            cols = slice(HD * h, HD * (h + 1))
            scores = lax.dot_general(
                queries[:, cols], kv[:, cols], (((1,), (1,)), ((), ())), preferred_element_type=F32
            )
            rows = scores.shape[0]
            tail = CAP - 128
            at = lax.broadcasted_iota(jnp.int32, (rows, 128), 1) + tail
            scores = jnp.concatenate(
                [scores[:, :tail], jnp.where(at < TOTAL, scores[:, tail:], MASKED)], axis=1
            )
            top = jnp.max(scores, axis=1, keepdims=True)
            weight = jnp.exp2((scores - top) * EXP2_SCALE)
            total = jnp.sum(weight, axis=1, keepdims=True)
            out = jnp.dot(weight.astype(BF16), vv[:, cols], preferred_element_type=F32)
            parts.append(jnp.where(live, out / total, 0.0).astype(BF16))
        return jnp.concatenate(parts, axis=1)

    def gates(g):
        lo = gav[:, pl.ds(mult(BLK * g, 128), BLK)]
        hi = gav[:, pl.ds(mult(HALF + BLK * g, 128), BLK)]
        return jnp.concatenate([lo, hi], axis=1)

    first, length = patch_at(0)
    for k in (1, 2, 3):
        md_copies[k].wait_recv()

    def prep0(n, carry):
        rows = pl.ds(mult(n * ROWS, ROWS), ROWS)
        heads(fh[rows, BLK:], rows)
        return carry

    lax.fori_loop(0, PATCH // ROWS, prep0, 0)
    ld_k.wait()
    ld_v.wait()
    refresh(first, length)

    def unit_rows(i):
        return pl.ds(mult(i * UNIT, UNIT), UNIT)

    def att1_copy(i):
        part = att1.at[pl.ds(mult(i * ROWS, ROWS), ROWS), own_cols]
        return remote(part, part, a1_s.at[i], a1_r.at[i], s, mate)

    def p1_copy(i, v):
        rows = unit_rows(i)
        return remote(sb1.at[v, rows], rb1.at[v, rows], p1_s.at[v, i], p1_r.at[v, i], pair, slab[v])

    def f1_copy(i):
        rows = unit_rows(i)
        return remote(fw1.at[rows], xs.at[rows], f1_s.at[i], f1_r.at[i], ahead, q)

    for copy in ld_res:
        copy.wait()
    for copy in res_copies:
        copy.wait_recv()
    for copy in ld_w[:4]:
        copy.wait()
    for copy in w_copies[:4]:
        copy.wait_recv()

    gate1 = [gates(slab[0]), gates(slab[1])]

    def step0(i, carry):
        @pl.when(i < PATCH // ROWS)
        def _():
            rows = pl.ds(mult(i * ROWS, ROWS), ROWS)
            live = lax.broadcasted_iota(jnp.int32, (ROWS, HD), 0) + i * ROWS < length
            att1[rows, own_cols] = attend(qb[rows, :], live)
            att1_copy(i).start()

        @pl.when(i > 0)
        def _():
            n = i - 1
            att1_copy(n).wait_recv()
            rows = pl.ds(mult(n * ROWS, ROWS), ROWS)
            live = lax.broadcasted_iota(jnp.int32, (ROWS, SLAB), 0) + n * ROWS < length
            keep = live & (n // 2 == j)
            for v in (0, 1):
                proj = jnp.dot(att1[rows, :], w4[slab[v]], preferred_element_type=F32)
                held = res[v, pl.ds(mult((n % 2) * ROWS, ROWS), ROWS), :].astype(F32)
                sb1[v, rows, :] = (proj * gate1[v] + jnp.where(keep, held, 0.0)).astype(BF16)
                for u in range(ROWS // UNIT):
                    p1_copy(n * (ROWS // UNIT) + u, v).start()

        return carry

    lax.fori_loop(0, PATCH // ROWS + 1, step0, 0)

    st2[0] = jnp.zeros((UNIT, 128), F32)
    lane = lax.broadcasted_iota(jnp.int32, (UNIT, 128), 1)

    def column_stats(i):
        hf = xs[unit_rows(i), :].astype(F32)
        mean = jnp.sum(hf, axis=1, keepdims=True) * (1.0 / SLAB)
        cent = hf - mean
        spread = jnp.sum(cent * cent, axis=1, keepdims=True)
        st2[0] = jnp.where(lane == 2 * i, mean, jnp.where(lane == 2 * i + 1, spread, st2[0]))

    def take(i, carry):
        @pl.when(i < UNITS)
        def _():
            for v in (0, 1):
                p1_copy(i, v).wait_recv()
            rows = unit_rows(i)
            held = (rb1[0, rows, :].astype(F32) + rb1[1, rows, :].astype(F32)).astype(BF16)

            @pl.when(even)
            def _():
                fw1[rows, :] = held
                f1_copy(i).start()

            @pl.when(jnp.logical_not(even))
            def _():
                xs[rows, :] = held
                column_stats(i)

        @pl.when((i >= LAG) & even)
        def _():
            f1_copy(i - LAG).wait_recv()
            column_stats(i - LAG)

        return carry

    lax.fori_loop(0, UNITS + LAG, take, 0)
    s2_copies = {}
    for k in (2, 3, 1):
        s2_copies[k] = remote(st2.at[0], st2.at[k], s2_s.at[k - 1], s2_r.at[k - 1], s, peer[k])
        s2_copies[k].start()
    rx_copies = []
    for v in (0, 1):
        src = xs.at[pl.ds(mult(ROWS * mate_slab[v], ROWS), ROWS)]
        copy = remote(src, rx.at[v], rx_s.at[v], rx_r.at[v], s, mate)
        copy.start()
        rx_copies.append(copy)

    first, length = patch_at(1)
    for k in (1, 2, 3):
        s2_copies[k].wait_recv()
    stats = [st2[k] for k in range(4)]
    total = stats[0] + stats[1] + stats[2] + stats[3]
    means = total * 0.25
    spread = pltpu.roll(total, 127, 1)
    for stat in stats:
        spread = spread + (stat - means) * (stat - means) * SLAB
    rstds = lax.rsqrt(spread * (1.0 / WIDTH) + EPS)
    for i in range(UNITS):
        rows = slice(i * UNIT, (i + 1) * UNIT)
        raw = xs[rows, :BLK].astype(F32)
        mean, rstd = means[:, 2 * i : 2 * i + 1], rstds[:, 2 * i : 2 * i + 1]
        modded = ((raw - mean) * rstd * scale_h + shift_h).astype(BF16)
        fh[rows, BLK:] = modded
        heads(modded, rows)

    refresh(first, length)

    def att2_copy(i):
        rows = pl.ds(mult(i * ROWS, ROWS), ROWS)
        return remote(as2.at[rows], att2.at[rows, own_cols], a2_s.at[i], a2_r.at[i], s, mate)

    def p2_copy(u, v):
        return remote(sb2.at[v, u], rb2.at[v, u], p2_s.at[v, u], p2_r.at[v, u], pair, slab[v])

    order = [c, 1 - c, 2 + c, 3 - c]

    def f2_copy(n, p, e):
        u = n * 4 + p
        return remote(
            fw2.at[u, :, pl.ds(e * BLK, BLK)],
            out_ref.at[unit_rows(n), block_cols(order[p], e)],
            f2_s.at[e, u],
            f2_r.at[e, u],
            ahead,
            q,
        )

    for copy in rx_copies:
        copy.wait_recv()
    for copy in ld_w[4:]:
        copy.wait()
    for copy in w_copies[4:]:
        copy.wait_recv()

    bases = [ROWS * slab[0], ROWS * slab[1], ROWS * mate_slab[0], ROWS * mate_slab[1]]

    def step1(i, carry):
        @pl.when(i < 2)
        def _():
            queries = jnp.concatenate(
                [qb[pl.ds(mult(base + UNIT * i, UNIT), UNIT), :] for base in bases], axis=0
            )
            r = lax.broadcasted_iota(jnp.int32, (4 * UNIT, HD), 0)
            seg = r // UNIT
            base = jnp.where(
                seg == 0, bases[0], jnp.where(seg == 1, bases[1], jnp.where(seg == 2, bases[2], bases[3]))
            )
            live = base + UNIT * i + r % UNIT < length
            got = attend(queries, live)
            rows = pl.ds(mult(i * ROWS, ROWS), ROWS)
            att2[rows, own_cols] = got[:ROWS]
            as2[rows, :] = got[ROWS:]
            att2_copy(i).start()

        @pl.when(i > 0)
        def _():
            n = i - 1
            att2_copy(n).wait_recv()
            rows = pl.ds(mult(n * ROWS, ROWS), ROWS)
            part = unit_rows(n)
            left = att2[rows, :]
            for p, g in enumerate(order):
                proj = jnp.dot(left, w4[g], preferred_element_type=F32) * gates(g)
                if p % 2 == 0:
                    held = jnp.concatenate(
                        [xs[pl.ds(mult(base + UNIT * n, UNIT), UNIT), :] for base in bases[:2]], axis=0
                    )
                else:
                    held = jnp.concatenate([rx[0, part, :], rx[1, part, :]], axis=0)
                proj = (proj + jnp.where(p // 2 == j, held.astype(F32), 0.0)).astype(BF16)
                for v in (0, 1):
                    sb2[v, n * 4 + p] = proj[v * UNIT : (v + 1) * UNIT]
                    p2_copy(n * 4 + p, v).start()

        return carry

    lax.fori_loop(0, 3, step1, 0)

    def finish(n, carry):
        for p, g in enumerate(order):
            u = n * 4 + p
            for v in (0, 1):
                p2_copy(u, v).wait_recv()
            held = (rb2[0, u].astype(F32) + rb2[1, u].astype(F32)).astype(BF16)

            @pl.when(even)
            def _():
                fw2[u] = held
                for e in (0, 1):
                    f2_copy(n, p, e).start()

            @pl.when(jnp.logical_not(even))
            def _():
                for e in (0, 1):
                    out_ref[unit_rows(n), block_cols(g, e)] = held[:, e * BLK : (e + 1) * BLK]

        return carry

    lax.fori_loop(0, 2, finish, 0)

    @pl.when(even)
    def _():
        for i in range(UNITS):
            f1_copy(i).wait_send()
        for n in range(2):
            for p in range(4):
                for e in (0, 1):
                    f2_copy(n, p, e).wait()

    for k in (1, 2, 3):
        md_copies[k].wait_send()
        s2_copies[k].wait_send()
    for copy in res_copies + w_copies + rx_copies:
        copy.wait_send()
    for i in range(PATCH // ROWS):
        att1_copy(i).wait_send()
    for i in range(UNITS):
        for v in (0, 1):
            p1_copy(i, v).wait_send()
            p2_copy(i, v).wait_send()
    for i in range(2):
        att2_copy(i).wait_send()


def shards(n_pipe, *args):
    dma = pltpu.SemaphoreType.DMA
    vmem = pltpu.VMEM
    any_space = pl.BlockSpec(memory_space=pl.ANY)
    smem = pl.BlockSpec(memory_space=pltpu.SMEM)
    chunks = PATCH // ROWS
    return pl.pallas_call(
        functools.partial(kernel, n_pipe),
        out_shape=jax.ShapeDtypeStruct((ROWS, WIDTH), BF16),
        in_specs=[any_space] * 9 + [smem] * 2,
        out_specs=pl.BlockSpec(memory_space=vmem),
        scratch_shapes=[
            vmem((ROWS, WIDTH), BF16),
            vmem((CAP, BLK), BF16),
            vmem((CAP, BLK), BF16),
            vmem((4, SLAB, SLAB), BF16),
            vmem((1, WIDTH), F32),
            vmem((1, WIDTH), F32),
            vmem((1, WIDTH), F32),
            vmem((1, HD), F32),
            vmem((1, HD), F32),
            vmem((ROWS, HALF), BF16),
            vmem((2, 2 * ROWS, SLAB), BF16),
            vmem((PATCH, BLK), BF16),
            vmem((PATCH, SLAB), BF16),
            vmem((PATCH, SLAB), BF16),
            vmem((2, PATCH, SLAB), BF16),
            vmem((2, PATCH, SLAB), BF16),
            vmem((PATCH, SLAB), BF16),
            vmem((PATCH, SLAB), BF16),
            vmem((4, UNIT, 128), F32),
            vmem((2, ROWS, SLAB), BF16),
            vmem((2 * ROWS, BLK), BF16),
            vmem((2 * ROWS, SLAB), BF16),
            vmem((2, UNITS, UNIT, SLAB), BF16),
            vmem((2, UNITS, UNIT, SLAB), BF16),
            vmem((UNITS, UNIT, SLAB), BF16),
            dma((20,)),
            dma((3,)),
            dma((3,)),
            dma((4,)),
            dma((4,)),
            dma((8,)),
            dma((8,)),
            dma((chunks,)),
            dma((chunks,)),
            dma((2, UNITS)),
            dma((2, UNITS)),
            dma((UNITS,)),
            dma((UNITS,)),
            dma((3,)),
            dma((3,)),
            dma((2,)),
            dma((2,)),
            dma((2,)),
            dma((2,)),
            dma((2, UNITS)),
            dma((2, UNITS)),
            dma((2, UNITS)),
            dma((2, UNITS)),
        ],
        compiler_params=pltpu.CompilerParams(
            collective_id=0, has_side_effects=True, vmem_limit_bytes=60 << 20
        ),
        name="section_steps",
    )(*args)


def solution(mesh):
    in_specs = (
        P(("pipe", "seq"), None),
        P("pipe", None, "seq"),
        P("pipe", None, "seq"),
        P("pipe", "seq", None),
        P("pipe", None),
        P("pipe", None),
        P("pipe", None),
        P("pipe", None),
        P("pipe", None),
        P(),
        P(),
    )
    return jax.shard_map(
        functools.partial(shards, mesh.shape["pipe"]),
        mesh=mesh,
        in_specs=in_specs,
        out_specs=P(("pipe", "seq"), None),
        check_vma=False,
    )
```

```python
import functools
import math

import jax
import jax.numpy as jnp
from jax import lax
from jax.experimental import pallas as pl
from jax.experimental.pallas import tpu as pltpu
from jax.sharding import PartitionSpec as P

MESH = pl.DeviceIdType.MESH
BF16 = jnp.bfloat16
F32 = jnp.float32

NP = 4
EPS = 1e-06
MASKED = -1e30
HD = 128
BLK = 384
SLAB = 2 * BLK
ROWS = 64
PATCH = 256
CAP = 1024
UNIT = 32
UNITS = PATCH // UNIT
CHUNK = 128
TOTAL = 960
WIDTH = 3072
HALF = WIDTH // 2
EXP2_SCALE = math.log2(math.e) / math.sqrt(HD)


def mult(value, of):
    return pl.multiple_of(value, of)


def kernel(
    n_pipe,
    x_hbm,
    k_hbm,
    v_hbm,
    w_hbm,
    shift_hbm,
    scale_hbm,
    gate_hbm,
    qg_hbm,
    kg_hbm,
    lengths_hbm,
    first_patch,
    out_ref,
    xv,
    kv,
    vv,
    w4,
    shv,
    scv,
    gav,
    qgv,
    kgv,
    md,
    res,
    qb,
    fh,
    att1,
    sb1,
    rb1,
    fw1,
    xs,
    st2,
    om,
    ml,
    rx,
    as2,
    att2,
    sb2,
    rb2,
    fw2,
    lengths,
    lsem,
    md_s,
    md_r,
    res_s,
    res_r,
    w_s,
    w_r,
    a1_s,
    a1_r,
    p1_s,
    p1_r,
    f1_s,
    f1_r,
    s2_s,
    s2_r,
    rx_s,
    rx_r,
    a2_s,
    a2_r,
    p2_s,
    p2_r,
    f2_s,
    f2_r,
):
    s = lax.axis_index("pipe")
    q = lax.axis_index("seq")
    j = q // 2
    c = q % 2
    odd = s % 2
    even = odd == 0
    pair = s + 1 - 2 * odd
    ahead = (s + 2) % n_pipe
    behind = (s + n_pipe - 2) % n_pipe
    chip = [j, 1 - j]
    slab = [2 * chip[0] + c, 2 * chip[1] + c]
    mate_slab = [2 * chip[0] + (1 - c), 2 * chip[1] + (1 - c)]
    peer = {1: mate_slab[0], 2: slab[1], 3: mate_slab[1]}
    mate = peer[1]
    own_rows = pl.ds(mult(ROWS * q, ROWS), ROWS)
    own_cols = pl.ds(mult(BLK * c, BLK), BLK)
    lane = lax.broadcasted_iota(jnp.int32, (ROWS, 128), 1)
    sub = lax.broadcasted_iota(jnp.int32, (ROWS, 128), 0)

    def block_cols(g, e):
        return pl.ds(mult(HALF * e + BLK * g, 128), BLK)

    def remote(src, dst, ssem, rsem, pipe, seq):
        return pltpu.make_async_remote_copy(
            src_ref=src,
            dst_ref=dst,
            send_sem=ssem,
            recv_sem=rsem,
            device_id={"pipe": pipe, "seq": seq},
            device_id_type=MESH,
        )

    bar = pltpu.get_barrier_semaphore()
    for k in (1, 2, 3):
        pl.semaphore_signal(bar, inc=1, device_id={"pipe": s, "seq": peer[k]}, device_id_type=MESH)
    for v in (0, 1):
        pl.semaphore_signal(bar, inc=1, device_id={"pipe": pair, "seq": slab[v]}, device_id_type=MESH)
    pl.semaphore_signal(bar, inc=1, device_id={"pipe": behind, "seq": q}, device_id_type=MESH)

    local = []

    def load(src, dst):
        copy = pltpu.make_async_copy(src, dst, lsem.at[len(local)])
        copy.start()
        local.append(copy)
        return copy

    ld_x = load(x_hbm, xv)
    ld_sc = load(scale_hbm, scv)
    ld_sh = load(shift_hbm, shv)
    ld_small = [load(gate_hbm, gav), load(qg_hbm, qgv), load(kg_hbm, kgv), load(lengths_hbm, lengths)]
    ld_k = load(k_hbm.at[0], kv)
    ld_v = load(v_hbm.at[0], vv)

    ld_x.wait()
    xf = xv[...].astype(F32)
    mean = jnp.sum(xf, axis=1, keepdims=True) * (1.0 / WIDTH)
    cent = xf - mean
    var = jnp.sum(cent * cent, axis=1, keepdims=True) * (1.0 / WIDTH)
    rstd = lax.rsqrt(var + EPS)
    ld_sc.wait()
    ld_sh.wait()
    md[...] = (
        (xv[:, :HALF].astype(F32) - mean) * rstd * (1.0 + scv[:, :HALF]) + shv[:, :HALF]
    ).astype(BF16)
    fh[own_rows, BLK:] = md[:, pl.ds(mult(BLK * q, 128), BLK)]

    pl.semaphore_wait(bar, 6)

    md_copies = {}
    for k in (2, 3, 1):
        md_copies[k] = remote(
            md.at[:, pl.ds(mult(BLK * peer[k], 128), BLK)],
            fh.at[own_rows, pl.ds(BLK, BLK)],
            md_s.at[k - 1],
            md_r.at[k - 1],
            s,
            peer[k],
        )
        md_copies[k].start()

    ld_res = []
    res_copies = []
    for v in (0, 1):
        for e in (0, 1):
            dst = res.at[v, pl.ds(mult(ROWS * c, ROWS), ROWS), pl.ds(BLK * e, BLK)]
            ld_res.append(load(x_hbm.at[:, block_cols(slab[v], e)], dst))
            copy = remote(
                x_hbm.at[:, block_cols(mate_slab[v], e)], dst, res_s.at[2 * v + e], res_r.at[2 * v + e], s, mate
            )
            copy.start()
            res_copies.append(copy)

    ld_w = []
    w_copies = []
    for n, (mine, his) in enumerate(
        [(slab[0], mate_slab[0]), (slab[1], mate_slab[1]), (mate_slab[0], slab[0]), (mate_slab[1], slab[1])]
    ):
        for e in (0, 1):
            for g, away in ((mine, False), (his, True)):
                src = w_hbm.at[0, :, block_cols(g, e)]
                dst = w4.at[g, own_cols, pl.ds(BLK * e, BLK)]
                if away:
                    copy = remote(src, dst, w_s.at[2 * n + e], w_r.at[2 * n + e], s, mate)
                    copy.start()
                    w_copies.append(copy)
                else:
                    ld_w.append(load(src, dst))

    for copy in ld_small:
        copy.wait()
    head_cols = pl.ds(mult(BLK * q, 128), BLK)
    scale_h = 1.0 + scv[:, head_cols]
    shift_h = shv[:, head_cols]
    q_gain = qgv[...]
    k_gain = kgv[...]

    def patch_at(t):
        p = (first_patch[0] + t + n_pipe * NP - s) % NP
        first = jnp.int32(0)
        length = jnp.int32(0)
        for n in range(NP):
            first = first + jnp.where(n < p, lengths[n], 0)
            length = length + jnp.where(n == p, lengths[n], 0)
        return first, length

    def heads(modded, rows):
        mf = modded.astype(F32)
        for h in range(BLK // HD):
            part = mf[:, HD * h : HD * (h + 1)]
            normed = part * lax.rsqrt(jnp.sum(part * part, axis=1, keepdims=True) * (1.0 / HD) + EPS)
            qb[rows, HD * h : HD * (h + 1)] = (normed * q_gain).astype(BF16)
            fh[rows, HD * h : HD * (h + 1)] = (normed * k_gain).astype(BF16)

    def refresh(first, length):
        def block(n, carry):
            rows = pl.ds(mult(n * PATCH, PATCH), PATCH)
            row = lax.broadcasted_iota(jnp.int32, (PATCH, PATCH), 0) + n * PATCH
            col = lax.broadcasted_iota(jnp.int32, (PATCH, PATCH), 1)
            pick = jnp.where((row - first == col) & (col < length), 1.0, 0.0).astype(BF16)
            placed = jnp.dot(pick, fh[...], preferred_element_type=F32)
            at = lax.broadcasted_iota(jnp.int32, (PATCH, BLK), 0) + n * PATCH
            inside = (at >= first) & (at < first + length)
            kv[rows, :] = jnp.where(inside, placed[:, :BLK], kv[rows, :].astype(F32)).astype(BF16)
            vv[rows, :] = jnp.where(inside, placed[:, BLK:], vv[rows, :].astype(F32)).astype(BF16)
            return carry

        lax.fori_loop(0, CAP // PATCH, block, 0)

    def stale_bias(first, length):
        at = lax.broadcasted_iota(jnp.int32, (1, CAP), 1)
        gone = ((at >= first) & (at < first + length)) | (at >= TOTAL)
        return jnp.where(gone, MASKED, 0.0)

    def stale_scores(queries, h, bias):
        cols = slice(HD * h, HD * (h + 1))
        return bias + lax.dot_general(
            queries[:, cols], kv[:, cols], (((1,), (1,)), ((), ())), preferred_element_type=F32
        )

    def fresh_scores(queries, h, length):
        cols = slice(HD * h, HD * (h + 1))
        scores = lax.dot_general(
            queries[:, cols], fh[:, cols], (((1,), (1,)), ((), ())), preferred_element_type=F32
        )
        at = lax.broadcasted_iota(jnp.int32, scores.shape, 1)
        return jnp.where(at < length, scores, MASKED)

    def weigh(scores, top):
        weight = jnp.exp2((scores - top) * EXP2_SCALE)
        return weight.astype(BF16), jnp.sum(weight, axis=1, keepdims=True)

    def stale_values(weight, h):
        return jnp.dot(weight, vv[:, HD * h : HD * (h + 1)], preferred_element_type=F32)

    def fresh_values(weight, h):
        cols = slice(BLK + HD * h, BLK + HD * (h + 1))
        return jnp.dot(weight, fh[:, cols], preferred_element_type=F32)

    heads_here = range(BLK // HD)

    def tops(scores):
        return [jnp.max(part, axis=1, keepdims=True) for part in scores]

    def attend(queries, live, bias, length):
        old = [stale_scores(queries, h, bias) for h in heads_here]
        new = [fresh_scores(queries, h, length) for h in heads_here]
        top = [jnp.maximum(a, b) for a, b in zip(tops(old), tops(new))]
        old = [weigh(part, m) for part, m in zip(old, top)]
        new = [weigh(part, m) for part, m in zip(new, top)]
        out = [stale_values(old[h][0], h) + fresh_values(new[h][0], h) for h in heads_here]
        return jnp.concatenate(
            [jnp.where(live, out[h] / (old[h][1] + new[h][1]), 0.0).astype(BF16) for h in heads_here], axis=1
        )

    def attend_stale(rows, bias):
        queries = qb[rows, :]
        scores = [stale_scores(queries, h, bias) for h in heads_here]
        top = tops(scores)
        old = [weigh(part, m) for part, m in zip(scores, top)]
        out = [stale_values(old[h][0], h) for h in heads_here]
        tile = jnp.zeros((ROWS, 128), F32)
        for h in heads_here:
            tile = jnp.where(lane == h, top[h], jnp.where(lane == 8 + h, old[h][1], tile))
        om[rows, :] = jnp.concatenate(out, axis=1)
        ml[rows, :] = tile

    def attend_fresh(queries, out, tile, live, length):
        scores = [fresh_scores(queries, h, length) for h in heads_here]
        old_top = [tile[:, h : h + 1] for h in heads_here]
        old_total = [tile[:, 8 + h : 9 + h] for h in heads_here]
        top = [jnp.maximum(a, b) for a, b in zip(old_top, tops(scores))]
        new = [weigh(part, m) for part, m in zip(scores, top)]
        shrink = [jnp.exp2((a - b) * EXP2_SCALE) for a, b in zip(old_top, top)]
        got = [
            out[:, HD * h : HD * (h + 1)] * shrink[h] + fresh_values(new[h][0], h) for h in heads_here
        ]
        return jnp.concatenate(
            [
                jnp.where(live, got[h] / (old_total[h] * shrink[h] + new[h][1]), 0.0).astype(BF16)
                for h in heads_here
            ],
            axis=1,
        )

    def gates(g):
        lo = gav[:, pl.ds(mult(BLK * g, 128), BLK)]
        hi = gav[:, pl.ds(mult(HALF + BLK * g, 128), BLK)]
        return jnp.concatenate([lo, hi], axis=1)

    first, length = patch_at(0)
    for k in (1, 2, 3):
        md_copies[k].wait_recv()

    def prep0(n, carry):
        rows = pl.ds(mult(n * ROWS, ROWS), ROWS)
        heads(fh[rows, BLK:], rows)
        return carry

    lax.fori_loop(0, PATCH // ROWS, prep0, 0)
    ld_k.wait()
    ld_v.wait()
    bias = stale_bias(first, length)
    next_first, next_length = patch_at(1)
    next_bias = stale_bias(next_first, next_length)

    def unit_rows(i):
        return pl.ds(mult(i * UNIT, UNIT), UNIT)

    def att1_copy(i):
        part = att1.at[pl.ds(mult(i * CHUNK, CHUNK), CHUNK), own_cols]
        return remote(part, part, a1_s.at[i], a1_r.at[i], s, mate)

    def p1_copy(i, v):
        rows = unit_rows(i)
        return remote(sb1.at[v, rows], rb1.at[v, rows], p1_s.at[v, i], p1_r.at[v, i], pair, slab[v])

    def f1_copy(i):
        rows = unit_rows(i)
        return remote(fw1.at[rows], xs.at[rows], f1_s.at[i], f1_r.at[i], ahead, q)

    for copy in ld_res:
        copy.wait()
    for copy in res_copies:
        copy.wait_recv()
    for copy in ld_w[:4]:
        copy.wait()
    for copy in w_copies[:4]:
        copy.wait_recv()

    gate1 = [gates(slab[0]), gates(slab[1])]

    def s2_copy(g, k):
        return remote(st2.at[0, g], st2.at[k, g], s2_s.at[k - 1, g], s2_r.at[k - 1, g], s, peer[k])

    def rx_copy(g):
        v = jnp.where(g // 2 == j, 0, 1)
        src = xs.at[pl.ds(mult(g * ROWS, ROWS), ROWS)]
        return remote(src, rx.at[v], rx_s.at[v], rx_r.at[v], s, mate)

    def ready(g):
        hf = xs[pl.ds(mult(g * ROWS, ROWS), ROWS), :].astype(F32)
        mean = jnp.sum(hf, axis=1, keepdims=True) * (1.0 / SLAB)
        cent = hf - mean
        spread = jnp.sum(cent * cent, axis=1, keepdims=True)
        tile = jnp.where(lane == sub, mean, jnp.where(lane == sub + ROWS, spread, 0.0))
        st2[0, g] = jnp.sum(tile, axis=0, keepdims=True)
        for k in (2, 3, 1):
            s2_copy(g, k).start()

        @pl.when(g % 2 != c)
        def _():
            rx_copy(g).start()

    def process(g):
        for k in (1, 2, 3):
            s2_copy(g, k).wait_recv()
        stats = [st2[k, g] for k in range(4)]
        total = stats[0] + stats[1] + stats[2] + stats[3]
        means = total * 0.25
        apart = jnp.zeros((1, 128), F32)
        for stat in stats:
            apart = apart + (stat - means) * (stat - means) * SLAB
        both = jnp.where(lane[:1] < ROWS, apart, total)
        mean = jnp.sum(jnp.where(lane == sub, means, 0.0), axis=1, keepdims=True)
        spread = jnp.sum(
            jnp.where((lane == sub) | (lane == sub + ROWS), both, 0.0), axis=1, keepdims=True
        )
        rstd = lax.rsqrt(spread * (1.0 / WIDTH) + EPS)
        rows = pl.ds(mult(g * ROWS, ROWS), ROWS)
        modded = ((xs[rows, :BLK].astype(F32) - mean) * rstd * scale_h + shift_h).astype(BF16)
        fh[rows, BLK:] = modded
        heads(modded, rows)
        attend_stale(rows, next_bias)

    def take(g):
        for u in range(ROWS // UNIT):
            i = g * (ROWS // UNIT) + u
            for v in (0, 1):
                p1_copy(i, v).wait_recv()
            rows = unit_rows(i)
            held = (rb1[0, rows, :].astype(F32) + rb1[1, rows, :].astype(F32)).astype(BF16)

            @pl.when(even)
            def _():
                fw1[rows, :] = held
                f1_copy(i).start()

            @pl.when(jnp.logical_not(even))
            def _():
                xs[rows, :] = held

    def taken(g):
        for u in range(ROWS // UNIT):
            f1_copy(g * (ROWS // UNIT) + u).wait_recv()

    groups = PATCH // ROWS

    def step0(i, carry):
        rows = pl.ds(mult(i * CHUNK, CHUNK), CHUNK)
        live = lax.broadcasted_iota(jnp.int32, (CHUNK, HD), 0) + i * CHUNK < length
        att1[rows, own_cols] = attend(qb[rows, :], live, bias, length)
        att1_copy(i).start()
        att1_copy(i).wait_recv()
        live = lax.broadcasted_iota(jnp.int32, (CHUNK, SLAB), 0) + i * CHUNK < length
        keep = live & (i == j)
        for v in (0, 1):
            proj = jnp.dot(att1[rows, :], w4[slab[v]], preferred_element_type=F32)
            held = res[v].astype(F32)
            sb1[v, rows, :] = (proj * gate1[v] + jnp.where(keep, held, 0.0)).astype(BF16)
            for u in range(CHUNK // UNIT):
                p1_copy(i * (CHUNK // UNIT) + u, v).start()
        return carry

    lax.fori_loop(0, PATCH // CHUNK, step0, 0)
    refresh(first, length)

    def hand_over(i, carry):
        @pl.when(i < groups)
        def _():
            take(i)

        @pl.when((i < groups) & jnp.logical_not(even))
        def _():
            ready(i)

        @pl.when((i >= 1) & (i < 1 + groups) & even)
        def _():
            taken(i - 1)
            ready(i - 1)

        done = i - 1 - (1 - odd)

        @pl.when((done >= 0) & (done < groups))
        def _():
            process(done)

        return carry

    lax.fori_loop(0, groups + 2, hand_over, 0)

    first, length = next_first, next_length

    def att2_copy(i):
        rows = pl.ds(mult(i * ROWS, ROWS), ROWS)
        return remote(as2.at[rows], att2.at[rows, own_cols], a2_s.at[i], a2_r.at[i], s, mate)

    def p2_copy(u, v):
        return remote(sb2.at[v, u], rb2.at[v, u], p2_s.at[v, u], p2_r.at[v, u], pair, slab[v])

    order = [c, 1 - c, 2 + c, 3 - c]

    def f2_copy(n, p, e):
        u = n * 4 + p
        return remote(
            fw2.at[u, :, pl.ds(e * BLK, BLK)],
            out_ref.at[unit_rows(n), block_cols(order[p], e)],
            f2_s.at[e, u],
            f2_r.at[e, u],
            ahead,
            q,
        )

    for v in (0, 1):
        rx_copy(mate_slab[v]).wait_recv()
    for copy in ld_w[4:]:
        copy.wait()
    for copy in w_copies[4:]:
        copy.wait_recv()

    bases = [ROWS * slab[0], ROWS * slab[1], ROWS * mate_slab[0], ROWS * mate_slab[1]]

    def finish(n):
        for p, g in enumerate(order):
            u = n * 4 + p
            for v in (0, 1):
                p2_copy(u, v).wait_recv()
            held = (rb2[0, u].astype(F32) + rb2[1, u].astype(F32)).astype(BF16)

            @pl.when(even)
            def _():
                fw2[u] = held
                for e in (0, 1):
                    f2_copy(n, p, e).start()

            @pl.when(jnp.logical_not(even))
            def _():
                for e in (0, 1):
                    out_ref[unit_rows(n), block_cols(g, e)] = held[:, e * BLK : (e + 1) * BLK]

    def step1(i, carry):
        @pl.when(i < 2)
        def _():
            queries = jnp.concatenate(
                [qb[pl.ds(mult(base + UNIT * i, UNIT), UNIT), :] for base in bases], axis=0
            )
            r = lax.broadcasted_iota(jnp.int32, (4 * UNIT, HD), 0)
            seg = r // UNIT
            base = jnp.where(
                seg == 0, bases[0], jnp.where(seg == 1, bases[1], jnp.where(seg == 2, bases[2], bases[3]))
            )
            live = base + UNIT * i + r % UNIT < length
            seen = [pl.ds(mult(base + UNIT * i, UNIT), UNIT) for base in bases]
            out = jnp.concatenate([om[part, :] for part in seen], axis=0)
            tile = jnp.concatenate([ml[part, :] for part in seen], axis=0)
            got = attend_fresh(queries, out, tile, live, length)
            rows = pl.ds(mult(i * ROWS, ROWS), ROWS)
            att2[rows, own_cols] = got[:ROWS]
            as2[rows, :] = got[ROWS:]
            att2_copy(i).start()

        @pl.when((i > 0) & (i < 3))
        def _():
            n = i - 1
            att2_copy(n).wait_recv()
            rows = pl.ds(mult(n * ROWS, ROWS), ROWS)
            part = unit_rows(n)
            left = att2[rows, :]
            for p, g in enumerate(order):
                proj = jnp.dot(left, w4[g], preferred_element_type=F32) * gates(g)
                if p % 2 == 0:
                    held = jnp.concatenate(
                        [xs[pl.ds(mult(base + UNIT * n, UNIT), UNIT), :] for base in bases[:2]], axis=0
                    )
                else:
                    held = jnp.concatenate([rx[0, part, :], rx[1, part, :]], axis=0)
                proj = (proj + jnp.where(p // 2 == j, held.astype(F32), 0.0)).astype(BF16)
                for v in (0, 1):
                    sb2[v, n * 4 + p] = proj[v * UNIT : (v + 1) * UNIT]
                    p2_copy(n * 4 + p, v).start()

        @pl.when(i > 1)
        def _():
            finish(i - 2)

        return carry

    lax.fori_loop(0, 4, step1, 0)

    @pl.when(even)
    def _():
        for i in range(UNITS):
            f1_copy(i).wait_send()
        for n in range(2):
            for p in range(4):
                for e in (0, 1):
                    f2_copy(n, p, e).wait()

    for k in (1, 2, 3):
        md_copies[k].wait_send()
        for g in range(groups):
            s2_copy(g, k).wait_send()
    for v in (0, 1):
        rx_copy(mate_slab[v]).wait_send()
    for copy in res_copies + w_copies:
        copy.wait_send()
    for i in range(PATCH // CHUNK):
        att1_copy(i).wait_send()
    for i in range(UNITS):
        for v in (0, 1):
            p1_copy(i, v).wait_send()
            p2_copy(i, v).wait_send()
    for i in range(2):
        att2_copy(i).wait_send()


def shards(n_pipe, *args):
    dma = pltpu.SemaphoreType.DMA
    vmem = pltpu.VMEM
    any_space = pl.BlockSpec(memory_space=pl.ANY)
    smem = pl.BlockSpec(memory_space=pltpu.SMEM)
    chunks = PATCH // ROWS
    held = [pltpu.with_memory_space_constraint(arg, pltpu.HBM) for arg in args[:10]]
    return pl.pallas_call(
        functools.partial(kernel, n_pipe),
        out_shape=jax.ShapeDtypeStruct((ROWS, WIDTH), BF16),
        in_specs=[any_space] * 10 + [smem],
        out_specs=pl.BlockSpec(memory_space=vmem),
        scratch_shapes=[
            vmem((ROWS, WIDTH), BF16),
            vmem((CAP, BLK), BF16),
            vmem((CAP, BLK), BF16),
            vmem((4, SLAB, SLAB), BF16),
            vmem((1, WIDTH), F32),
            vmem((1, WIDTH), F32),
            vmem((1, WIDTH), F32),
            vmem((1, HD), F32),
            vmem((1, HD), F32),
            vmem((ROWS, HALF), BF16),
            vmem((2, 2 * ROWS, SLAB), BF16),
            vmem((PATCH, BLK), BF16),
            vmem((PATCH, SLAB), BF16),
            vmem((PATCH, SLAB), BF16),
            vmem((2, PATCH, SLAB), BF16),
            vmem((2, PATCH, SLAB), BF16),
            vmem((PATCH, SLAB), BF16),
            vmem((PATCH, SLAB), BF16),
            vmem((4, chunks, 1, 128), F32),
            vmem((PATCH, BLK), F32),
            vmem((PATCH, 128), F32),
            vmem((2, ROWS, SLAB), BF16),
            vmem((2 * ROWS, BLK), BF16),
            vmem((2 * ROWS, SLAB), BF16),
            vmem((2, UNITS, UNIT, SLAB), BF16),
            vmem((2, UNITS, UNIT, SLAB), BF16),
            vmem((UNITS, UNIT, SLAB), BF16),
            pltpu.SMEM((NP,), jnp.int32),
            dma((21,)),
            dma((3,)),
            dma((3,)),
            dma((4,)),
            dma((4,)),
            dma((8,)),
            dma((8,)),
            dma((PATCH // CHUNK,)),
            dma((PATCH // CHUNK,)),
            dma((2, UNITS)),
            dma((2, UNITS)),
            dma((UNITS,)),
            dma((UNITS,)),
            dma((3, chunks)),
            dma((3, chunks)),
            dma((2,)),
            dma((2,)),
            dma((2,)),
            dma((2,)),
            dma((2, UNITS)),
            dma((2, UNITS)),
            dma((2, UNITS)),
            dma((2, UNITS)),
        ],
        compiler_params=pltpu.CompilerParams(
            collective_id=0, has_side_effects=True, vmem_limit_bytes=40 << 20
        ),
        name="section_steps",
    )(*held, args[10])


def solution(mesh):
    in_specs = (
        P(("pipe", "seq"), None),
        P("pipe", None, "seq"),
        P("pipe", None, "seq"),
        P("pipe", "seq", None),
        P("pipe", None),
        P("pipe", None),
        P("pipe", None),
        P("pipe", None),
        P("pipe", None),
        P(),
        P(),
    )
    return jax.shard_map(
        functools.partial(shards, mesh.shape["pipe"]),
        mesh=mesh,
        in_specs=in_specs,
        out_specs=P(("pipe", "seq"), None),
        check_vma=False,
    )
```

```python
import functools
import math

import jax
import jax.numpy as jnp
from jax import lax
from jax.experimental import pallas as pl
from jax.experimental.pallas import tpu as pltpu
from jax.sharding import PartitionSpec as P

MESH = pl.DeviceIdType.MESH
BF16 = jnp.bfloat16
F32 = jnp.float32

NP = 4
EPS = 1e-06
MASKED = -1e30
HD = 128
BLK = 384
SLAB = 2 * BLK
ROWS = 64
PATCH = 256
CAP = 1024
UNIT = 32
UNITS = PATCH // UNIT
UNIT1 = 32
UNITS1 = PATCH // UNIT1
BEHIND = 2
CHUNK = 128
TOTAL = 960
WIDTH = 3072
HALF = WIDTH // 2
EXP2_SCALE = math.log2(math.e) / math.sqrt(HD)


def mult(value, of):
    return pl.multiple_of(value, of)


def kernel(
    n_pipe,
    x_hbm,
    k_hbm,
    v_hbm,
    w_hbm,
    shift_hbm,
    scale_hbm,
    gate_hbm,
    qg_hbm,
    kg_hbm,
    lengths_hbm,
    first_patch,
    out_ref,
    xv,
    kv,
    vv,
    w4,
    shv,
    scv,
    gav,
    qgv,
    kgv,
    md,
    res,
    qb,
    fh,
    att1,
    sb1,
    rb1,
    fw1,
    xs,
    st2,
    om,
    ml,
    rx,
    as2,
    att2,
    sb2,
    rb2,
    fw2,
    lengths,
    lsem,
    md_s,
    md_r,
    res_s,
    res_r,
    w_s,
    w_r,
    a1_s,
    a1_r,
    p1_s,
    p1_r,
    f1_s,
    f1_r,
    s2_s,
    s2_r,
    rx_s,
    rx_r,
    a2_s,
    a2_r,
    p2_s,
    p2_r,
    f2_s,
    f2_r,
):
    s = lax.axis_index("pipe")
    q = lax.axis_index("seq")
    j = q // 2
    c = q % 2
    odd = s % 2
    even = odd == 0
    pair = s + 1 - 2 * odd
    ahead = (s + 2) % n_pipe
    behind = (s + n_pipe - 2) % n_pipe
    chip = [j, 1 - j]
    slab = [2 * chip[0] + c, 2 * chip[1] + c]
    mate_slab = [2 * chip[0] + (1 - c), 2 * chip[1] + (1 - c)]
    peer = {1: mate_slab[0], 2: slab[1], 3: mate_slab[1]}
    mate = peer[1]
    own_rows = pl.ds(mult(ROWS * q, ROWS), ROWS)
    own_cols = pl.ds(mult(BLK * c, BLK), BLK)
    lane = lax.broadcasted_iota(jnp.int32, (ROWS, 128), 1)
    sub = lax.broadcasted_iota(jnp.int32, (ROWS, 128), 0)

    def block_cols(g, e):
        return pl.ds(mult(HALF * e + BLK * g, 128), BLK)

    def remote(src, dst, ssem, rsem, pipe, seq):
        return pltpu.make_async_remote_copy(
            src_ref=src,
            dst_ref=dst,
            send_sem=ssem,
            recv_sem=rsem,
            device_id={"pipe": pipe, "seq": seq},
            device_id_type=MESH,
        )

    bar = pltpu.get_barrier_semaphore()
    for k in (1, 2, 3):
        pl.semaphore_signal(bar, inc=1, device_id={"pipe": s, "seq": peer[k]}, device_id_type=MESH)
    for v in (0, 1):
        pl.semaphore_signal(bar, inc=1, device_id={"pipe": pair, "seq": slab[v]}, device_id_type=MESH)
    pl.semaphore_signal(bar, inc=1, device_id={"pipe": behind, "seq": q}, device_id_type=MESH)

    local = []

    def load(src, dst):
        copy = pltpu.make_async_copy(src, dst, lsem.at[len(local)])
        copy.start()
        local.append(copy)
        return copy

    ld_x = load(x_hbm, xv)
    ld_sc = load(scale_hbm, scv)
    ld_sh = load(shift_hbm, shv)
    ld_small = [load(gate_hbm, gav), load(qg_hbm, qgv), load(kg_hbm, kgv), load(lengths_hbm, lengths)]
    ld_k = load(k_hbm.at[0], kv)
    ld_v = load(v_hbm.at[0], vv)

    ld_x.wait()
    xf = xv[...].astype(F32)
    mean = jnp.sum(xf, axis=1, keepdims=True) * (1.0 / WIDTH)
    cent = xf - mean
    var = jnp.sum(cent * cent, axis=1, keepdims=True) * (1.0 / WIDTH)
    rstd = lax.rsqrt(var + EPS)
    ld_sc.wait()
    ld_sh.wait()
    md[...] = (
        (xv[:, :HALF].astype(F32) - mean) * rstd * (1.0 + scv[:, :HALF]) + shv[:, :HALF]
    ).astype(BF16)
    fh[own_rows, BLK:] = md[:, pl.ds(mult(BLK * q, 128), BLK)]

    for copy in ld_small:
        copy.wait()
    head_cols = pl.ds(mult(BLK * q, 128), BLK)
    scale_h = 1.0 + scv[:, head_cols]
    shift_h = shv[:, head_cols]
    q_gain = qgv[...]
    k_gain = kgv[...]

    def heads(modded, rows):
        mf = modded.astype(F32)
        for h in range(BLK // HD):
            part = mf[:, HD * h : HD * (h + 1)]
            normed = part * lax.rsqrt(jnp.sum(part * part, axis=1, keepdims=True) * (1.0 / HD) + EPS)
            qb[rows, HD * h : HD * (h + 1)] = (normed * q_gain).astype(BF16)
            fh[rows, HD * h : HD * (h + 1)] = (normed * k_gain).astype(BF16)

    heads(fh[own_rows, BLK:], own_rows)
    pl.semaphore_wait(bar, 6)

    md_copies = {}
    for k in (2, 3, 1):
        md_copies[k] = remote(
            md.at[:, pl.ds(mult(BLK * peer[k], 128), BLK)],
            fh.at[own_rows, pl.ds(BLK, BLK)],
            md_s.at[k - 1],
            md_r.at[k - 1],
            s,
            peer[k],
        )
        md_copies[k].start()

    ld_res = []
    res_copies = []
    for v in (0, 1):
        for e in (0, 1):
            dst = res.at[v, pl.ds(mult(ROWS * c, ROWS), ROWS), pl.ds(BLK * e, BLK)]
            ld_res.append(load(x_hbm.at[:, block_cols(slab[v], e)], dst))
            copy = remote(
                x_hbm.at[:, block_cols(mate_slab[v], e)], dst, res_s.at[2 * v + e], res_r.at[2 * v + e], s, mate
            )
            copy.start()
            res_copies.append(copy)

    ld_w = []
    w_copies = []
    for n, (mine, his) in enumerate(
        [(slab[0], mate_slab[0]), (slab[1], mate_slab[1]), (mate_slab[0], slab[0]), (mate_slab[1], slab[1])]
    ):
        for e in (0, 1):
            for g, away in ((mine, False), (his, True)):
                src = w_hbm.at[0, :, block_cols(g, e)]
                dst = w4.at[g, own_cols, pl.ds(BLK * e, BLK)]
                if away:
                    copy = remote(src, dst, w_s.at[2 * n + e], w_r.at[2 * n + e], s, mate)
                    copy.start()
                    w_copies.append(copy)
                else:
                    ld_w.append(load(src, dst))

    def patch_at(t):
        p = (first_patch[0] + t + n_pipe * NP - s) % NP
        first = jnp.int32(0)
        length = jnp.int32(0)
        for n in range(NP):
            first = first + jnp.where(n < p, lengths[n], 0)
            length = length + jnp.where(n == p, lengths[n], 0)
        return first, length

    def refresh(first, length):
        def block(n, carry):
            rows = pl.ds(mult(n * PATCH, PATCH), PATCH)
            row = lax.broadcasted_iota(jnp.int32, (PATCH, PATCH), 0) + n * PATCH
            col = lax.broadcasted_iota(jnp.int32, (PATCH, PATCH), 1)
            pick = jnp.where((row - first == col) & (col < length), 1.0, 0.0).astype(BF16)
            placed = jnp.dot(pick, fh[...], preferred_element_type=F32)
            at = lax.broadcasted_iota(jnp.int32, (PATCH, BLK), 0) + n * PATCH
            inside = (at >= first) & (at < first + length)
            kv[rows, :] = jnp.where(inside, placed[:, :BLK], kv[rows, :].astype(F32)).astype(BF16)
            vv[rows, :] = jnp.where(inside, placed[:, BLK:], vv[rows, :].astype(F32)).astype(BF16)
            return carry

        lax.fori_loop(0, CAP // PATCH, block, 0)

    def stale_bias(first, length):
        at = lax.broadcasted_iota(jnp.int32, (1, CAP), 1)
        gone = ((at >= first) & (at < first + length)) | (at >= TOTAL)
        return jnp.where(gone, MASKED, 0.0)

    def stale_scores(queries, h, bias):
        cols = slice(HD * h, HD * (h + 1))
        return bias + lax.dot_general(
            queries[:, cols], kv[:, cols], (((1,), (1,)), ((), ())), preferred_element_type=F32
        )

    def fresh_scores(queries, h, length):
        cols = slice(HD * h, HD * (h + 1))
        scores = lax.dot_general(
            queries[:, cols], fh[:, cols], (((1,), (1,)), ((), ())), preferred_element_type=F32
        )
        at = lax.broadcasted_iota(jnp.int32, scores.shape, 1)
        return jnp.where(at < length, scores, MASKED)

    def weigh(scores, top):
        weight = jnp.exp2((scores - top) * EXP2_SCALE)
        return weight.astype(BF16), jnp.sum(weight, axis=1, keepdims=True)

    def stale_values(weight, h):
        return jnp.dot(weight, vv[:, HD * h : HD * (h + 1)], preferred_element_type=F32)

    def fresh_values(weight, h):
        cols = slice(BLK + HD * h, BLK + HD * (h + 1))
        return jnp.dot(weight, fh[:, cols], preferred_element_type=F32)

    heads_here = range(BLK // HD)

    def tops(scores):
        return [jnp.max(part, axis=1, keepdims=True) for part in scores]

    def attend(queries, live, bias, length):
        old = [stale_scores(queries, h, bias) for h in heads_here]
        new = [fresh_scores(queries, h, length) for h in heads_here]
        top = [jnp.maximum(a, b) for a, b in zip(tops(old), tops(new))]
        old = [weigh(part, m) for part, m in zip(old, top)]
        new = [weigh(part, m) for part, m in zip(new, top)]
        out = [stale_values(old[h][0], h) + fresh_values(new[h][0], h) for h in heads_here]
        return jnp.concatenate(
            [jnp.where(live, out[h] / (old[h][1] + new[h][1]), 0.0).astype(BF16) for h in heads_here], axis=1
        )

    def soften(scores, values):
        top = tops(scores)
        weight = [weigh(part, m) for part, m in zip(scores, top)]
        return top, [part[1] for part in weight], [values(weight[h][0], h) for h in heads_here]

    def keep_stale(rows, top, total, out):
        tile = jnp.zeros((ROWS, 128), F32)
        for h in heads_here:
            tile = jnp.where(lane == h, top[h], jnp.where(lane == 8 + h, total[h], tile))
        om[rows, :] = jnp.concatenate(out, axis=1)
        ml[rows, :] = tile

    def attend_stale(rows, bias):
        queries = qb[rows, :]
        keep_stale(rows, *soften([stale_scores(queries, h, bias) for h in heads_here], stale_values))

    def merge_parts(out, tile, fresh, live):
        parts = []
        for h, (top, total, got) in enumerate(zip(*fresh)):
            old_top, old_total = tile[:, h : h + 1], tile[:, 8 + h : 9 + h]
            both = jnp.maximum(old_top, top)
            a = jnp.exp2((old_top - both) * EXP2_SCALE)
            b = jnp.exp2((top - both) * EXP2_SCALE)
            got = out[:, HD * h : HD * (h + 1)] * a + got * b
            parts.append(jnp.where(live, got / (old_total * a + total * b), 0.0).astype(BF16))
        return jnp.concatenate(parts, axis=1)

    def gates(g):
        lo = gav[:, pl.ds(mult(BLK * g, 128), BLK)]
        hi = gav[:, pl.ds(mult(HALF + BLK * g, 128), BLK)]
        return jnp.concatenate([lo, hi], axis=1)

    first, length = patch_at(0)
    for k in (1, 2, 3):
        md_copies[k].wait_recv()
        rows = pl.ds(mult(ROWS * peer[k], ROWS), ROWS)
        heads(fh[rows, BLK:], rows)
    ld_k.wait()
    ld_v.wait()
    bias = stale_bias(first, length)
    next_first, next_length = patch_at(1)
    next_bias = stale_bias(next_first, next_length)

    def unit_rows(i):
        return pl.ds(mult(i * UNIT, UNIT), UNIT)

    def unit1_rows(i):
        return pl.ds(mult(i * UNIT1, UNIT1), UNIT1)

    def att1_copy(i):
        part = att1.at[pl.ds(mult(i * CHUNK, CHUNK), CHUNK), own_cols]
        return remote(part, part, a1_s.at[i], a1_r.at[i], s, mate)

    def p1_copy(i, v):
        rows = unit1_rows(i)
        return remote(sb1.at[v, rows], rb1.at[v, rows], p1_s.at[v, i], p1_r.at[v, i], pair, slab[v])

    def f1_copy(i):
        rows = unit1_rows(i)
        return remote(fw1.at[rows], xs.at[rows], f1_s.at[i], f1_r.at[i], ahead, q)

    for copy in ld_res:
        copy.wait()
    for copy in res_copies:
        copy.wait_recv()
    for copy in ld_w[:4]:
        copy.wait()
    for copy in w_copies[:4]:
        copy.wait_recv()

    gate1 = [gates(slab[0]), gates(slab[1])]

    def s2_copy(g, k):
        return remote(st2.at[0, g], st2.at[k, g], s2_s.at[k - 1, g], s2_r.at[k - 1, g], s, peer[k])

    def rx_copy(g):
        v = jnp.where(g // 2 == j, 0, 1)
        src = xs.at[pl.ds(mult(g * ROWS, ROWS), ROWS)]
        return remote(src, rx.at[v], rx_s.at[v], rx_r.at[v], s, mate)

    def ready(g):
        hf = xs[pl.ds(mult(g * ROWS, ROWS), ROWS), :].astype(F32)
        mean = jnp.sum(hf, axis=1, keepdims=True) * (1.0 / SLAB)
        cent = hf - mean
        spread = jnp.sum(cent * cent, axis=1, keepdims=True)
        tile = jnp.where(lane == sub, mean, jnp.where(lane == sub + ROWS, spread, 0.0))
        st2[0, g] = jnp.sum(tile, axis=0, keepdims=True)
        for k in (2, 3, 1):
            s2_copy(g, k).start()

        @pl.when(g % 2 != c)
        def _():
            rx_copy(g).start()

    def process(g):
        for k in (1, 2, 3):
            s2_copy(g, k).wait_recv()
        stats = [st2[k, g] for k in range(4)]
        total = stats[0] + stats[1] + stats[2] + stats[3]
        means = total * 0.25
        apart = jnp.zeros((1, 128), F32)
        for stat in stats:
            apart = apart + (stat - means) * (stat - means) * SLAB
        both = jnp.where(lane[:1] < ROWS, apart, total)
        mean = jnp.sum(jnp.where(lane == sub, means, 0.0), axis=1, keepdims=True)
        spread = jnp.sum(
            jnp.where((lane == sub) | (lane == sub + ROWS), both, 0.0), axis=1, keepdims=True
        )
        rstd = lax.rsqrt(spread * (1.0 / WIDTH) + EPS)
        rows = pl.ds(mult(g * ROWS, ROWS), ROWS)
        modded = ((xs[rows, :BLK].astype(F32) - mean) * rstd * scale_h + shift_h).astype(BF16)
        fh[rows, BLK:] = modded
        heads(modded, rows)

        @pl.when(g < groups - 1)
        def _():
            attend_stale(rows, next_bias)

    def take(g):
        for u in range(ROWS // UNIT1):
            i = g * (ROWS // UNIT1) + u
            for v in (0, 1):
                p1_copy(i, v).wait_recv()
            rows = unit1_rows(i)
            held = (rb1[0, rows, :].astype(F32) + rb1[1, rows, :].astype(F32)).astype(BF16)

            @pl.when(even)
            def _():
                fw1[rows, :] = held
                f1_copy(i).start()

            @pl.when(jnp.logical_not(even))
            def _():
                xs[rows, :] = held

    def taken(g):
        for u in range(ROWS // UNIT1):
            f1_copy(g * (ROWS // UNIT1) + u).wait_recv()

    groups = PATCH // ROWS

    def step0(i, carry):
        rows = pl.ds(mult(i * CHUNK, CHUNK), CHUNK)
        live = lax.broadcasted_iota(jnp.int32, (CHUNK, HD), 0) + i * CHUNK < length
        att1[rows, own_cols] = attend(qb[rows, :], live, bias, length)
        att1_copy(i).start()
        att1_copy(i).wait_recv()
        live = lax.broadcasted_iota(jnp.int32, (CHUNK, SLAB), 0) + i * CHUNK < length
        keep = live & (i == j)
        for v in (0, 1):
            proj = jnp.dot(att1[rows, :], w4[slab[v]], preferred_element_type=F32)
            held = res[v].astype(F32)
            sb1[v, rows, :] = (proj * gate1[v] + jnp.where(keep, held, 0.0)).astype(BF16)
            for u in range(CHUNK // UNIT1):
                p1_copy(i * (CHUNK // UNIT1) + u, v).start()
        return carry

    lax.fori_loop(0, PATCH // CHUNK, step0, 0)
    refresh(first, length)

    def hand_over(i, carry):
        @pl.when(i < groups)
        def _():
            take(i)

        @pl.when((i < groups) & jnp.logical_not(even))
        def _():
            ready(i)

        @pl.when((i >= 1) & (i < 1 + groups) & even)
        def _():
            taken(i - 1)
            ready(i - 1)

        done = i - 1 - (1 - odd)

        @pl.when((done >= 0) & (done < groups))
        def _():
            process(done)

        return carry

    lax.fori_loop(0, groups + 2, hand_over, 0)

    first, length = next_first, next_length

    def att2_copy(i):
        rows = pl.ds(mult(i * ROWS, ROWS), ROWS)
        return remote(as2.at[rows], att2.at[rows, own_cols], a2_s.at[i], a2_r.at[i], s, mate)

    def slab_of(u):
        p = u % 4
        return 2 * (p // 2) + (c + p % 2) % 2

    def p2_copy(u, e, v):
        return remote(sb2.at[v, u, e], rb2.at[v, u, e], p2_s.at[v, u, e], p2_r.at[v, u, e], pair, slab[v])

    def f2_copy(u, e):
        dst = out_ref.at[unit_rows(u // 4), block_cols(slab_of(u), e)]
        return remote(fw2.at[u, e], dst, f2_s.at[u, e], f2_r.at[u, e], ahead, q)

    for v in (0, 1):
        rx_copy(mate_slab[v]).wait_recv()
    for copy in ld_w[4:]:
        copy.wait()
    for copy in w_copies[4:]:
        copy.wait_recv()

    bases = [ROWS * slab[0], ROWS * slab[1], ROWS * mate_slab[0], ROWS * mate_slab[1]]

    def finish(u):
        for e in (0, 1):
            for v in (0, 1):
                p2_copy(u, e, v).wait_recv()
            held = (rb2[0, u, e].astype(F32) + rb2[1, u, e].astype(F32)).astype(BF16)

            @pl.when(even)
            def _():
                fw2[u, e] = held
                f2_copy(u, e).start()

            @pl.when(jnp.logical_not(even))
            def _():
                out_ref[unit_rows(u // 4), block_cols(slab_of(u), e)] = held

    r = lax.broadcasted_iota(jnp.int32, (4 * UNIT, HD), 0)
    seg = r // UNIT
    start = jnp.where(
        seg == 0, bases[0], jnp.where(seg == 1, bases[1], jnp.where(seg == 2, bases[2], bases[3]))
    )

    def merge(i, last=None):
        seen = [pl.ds(mult(base + UNIT * i, UNIT), UNIT) for base in bases]
        queries = jnp.concatenate([qb[part, :] for part in seen], axis=0)
        new = [fresh_scores(queries, h, length) for h in heads_here]
        if last is None:
            fresh = soften(new, fresh_values)
        else:
            late = qb[last, :]
            old = [stale_scores(late, h, next_bias) for h in heads_here]
            old_top, new_top = tops(old), tops(new)
            old = [weigh(part, m) for part, m in zip(old, old_top)]
            new = [weigh(part, m) for part, m in zip(new, new_top)]
            old_out = [stale_values(old[h][0], h) for h in heads_here]
            fresh = new_top, [part[1] for part in new], [fresh_values(new[h][0], h) for h in heads_here]
            keep_stale(last, old_top, [part[1] for part in old], old_out)
        out = jnp.concatenate([om[part, :] for part in seen], axis=0)
        tile = jnp.concatenate([ml[part, :] for part in seen], axis=0)
        live = start + UNIT * i + r % UNIT < length
        got = merge_parts(out, tile, fresh, live)
        rows = pl.ds(i * ROWS, ROWS)
        att2[rows, own_cols] = got[:ROWS]
        as2[rows, :] = got[ROWS:]
        att2_copy(i).start()

    merge(0, pl.ds(PATCH - ROWS, ROWS))
    merge(1)

    def step1(u, carry):
        n = u // 4
        p = u % 4

        @pl.when(p == 0)
        def _():
            att2_copy(n).wait_recv()

        @pl.when(u < UNITS)
        def _():
            g = slab_of(u)
            part = unit_rows(n)
            left = att2[pl.ds(mult(n * ROWS, ROWS), ROWS), :]
            proj = jnp.dot(left, w4[g], preferred_element_type=F32) * gates(g)
            own = jnp.concatenate(
                [xs[pl.ds(mult(base + UNIT * n, UNIT), UNIT), :] for base in bases[:2]], axis=0
            )
            his = jnp.concatenate([rx[0, part, :], rx[1, part, :]], axis=0)
            held = jnp.where(p % 2 == 0, own.astype(F32), his.astype(F32))
            proj = (proj + jnp.where(p // 2 == j, held, 0.0)).astype(BF16)
            for v in (0, 1):
                for e in (0, 1):
                    sb2[v, u, e] = proj[v * UNIT : (v + 1) * UNIT, e * BLK : (e + 1) * BLK]
                    p2_copy(u, e, v).start()

        @pl.when((u >= BEHIND) & even)
        def _():
            finish(u - BEHIND)

        return carry

    lax.fori_loop(0, UNITS, step1, 0)

    def rest(u, carry):
        @pl.when((u >= UNITS - BEHIND) | jnp.logical_not(even))
        def _():
            finish(u)

        return carry

    lax.fori_loop(0, UNITS, rest, 0)

    @pl.when(even)
    def _():
        for i in range(UNITS1):
            f1_copy(i).wait_send()
        for u in range(UNITS):
            for e in (0, 1):
                f2_copy(u, e).wait()

    for k in (1, 2, 3):
        md_copies[k].wait_send()
        for g in range(groups):
            s2_copy(g, k).wait_send()
    for v in (0, 1):
        rx_copy(mate_slab[v]).wait_send()
    for copy in res_copies + w_copies:
        copy.wait_send()
    for i in range(PATCH // CHUNK):
        att1_copy(i).wait_send()
    for i in range(UNITS1):
        for v in (0, 1):
            p1_copy(i, v).wait_send()
    for u in range(UNITS):
        for v in (0, 1):
            for e in (0, 1):
                p2_copy(u, e, v).wait_send()
    for i in range(2):
        att2_copy(i).wait_send()


def shards(n_pipe, *args):
    dma = pltpu.SemaphoreType.DMA
    vmem = pltpu.VMEM
    any_space = pl.BlockSpec(memory_space=pl.ANY)
    smem = pl.BlockSpec(memory_space=pltpu.SMEM)
    chunks = PATCH // ROWS
    held = [pltpu.with_memory_space_constraint(arg, pltpu.HBM) for arg in args[:10]]
    return pl.pallas_call(
        functools.partial(kernel, n_pipe),
        out_shape=jax.ShapeDtypeStruct((ROWS, WIDTH), BF16),
        in_specs=[any_space] * 10 + [smem],
        out_specs=pl.BlockSpec(memory_space=vmem),
        scratch_shapes=[
            vmem((ROWS, WIDTH), BF16),
            vmem((CAP, BLK), BF16),
            vmem((CAP, BLK), BF16),
            vmem((4, SLAB, SLAB), BF16),
            vmem((1, WIDTH), F32),
            vmem((1, WIDTH), F32),
            vmem((1, WIDTH), F32),
            vmem((1, HD), F32),
            vmem((1, HD), F32),
            vmem((ROWS, HALF), BF16),
            vmem((2, 2 * ROWS, SLAB), BF16),
            vmem((PATCH, BLK), BF16),
            vmem((PATCH, SLAB), BF16),
            vmem((PATCH, SLAB), BF16),
            vmem((2, PATCH, SLAB), BF16),
            vmem((2, PATCH, SLAB), BF16),
            vmem((PATCH, SLAB), BF16),
            vmem((PATCH, SLAB), BF16),
            vmem((4, chunks, 1, 128), F32),
            vmem((PATCH, BLK), F32),
            vmem((PATCH, 128), F32),
            vmem((2, ROWS, SLAB), BF16),
            vmem((2 * ROWS, BLK), BF16),
            vmem((2 * ROWS, SLAB), BF16),
            vmem((2, UNITS, 2, UNIT, BLK), BF16),
            vmem((2, UNITS, 2, UNIT, BLK), BF16),
            vmem((UNITS, 2, UNIT, BLK), BF16),
            pltpu.SMEM((NP,), jnp.int32),
            dma((21,)),
            dma((3,)),
            dma((3,)),
            dma((4,)),
            dma((4,)),
            dma((8,)),
            dma((8,)),
            dma((PATCH // CHUNK,)),
            dma((PATCH // CHUNK,)),
            dma((2, UNITS1)),
            dma((2, UNITS1)),
            dma((UNITS1,)),
            dma((UNITS1,)),
            dma((3, chunks)),
            dma((3, chunks)),
            dma((2,)),
            dma((2,)),
            dma((2,)),
            dma((2,)),
            dma((2, UNITS, 2)),
            dma((2, UNITS, 2)),
            dma((UNITS, 2)),
            dma((UNITS, 2)),
        ],
        compiler_params=pltpu.CompilerParams(
            collective_id=0, has_side_effects=True, vmem_limit_bytes=40 << 20
        ),
        name="section_steps",
    )(*held, args[10])


def solution(mesh):
    in_specs = (
        P(("pipe", "seq"), None),
        P("pipe", None, "seq"),
        P("pipe", None, "seq"),
        P("pipe", "seq", None),
        P("pipe", None),
        P("pipe", None),
        P("pipe", None),
        P("pipe", None),
        P("pipe", None),
        P(),
        P(),
    )
    return jax.shard_map(
        functools.partial(shards, mesh.shape["pipe"]),
        mesh=mesh,
        in_specs=in_specs,
        out_specs=P(("pipe", "seq"), None),
        check_vma=False,
    )
```

```python
import functools
import math

import jax
import jax.numpy as jnp
from jax import lax
from jax.experimental import pallas as pl
from jax.experimental.pallas import tpu as pltpu
from jax.sharding import PartitionSpec as P

MESH = pl.DeviceIdType.MESH
BF16 = jnp.bfloat16
F32 = jnp.float32

NP = 4
EPS = 1e-06
MASKED = -1e30
HD = 128
BLK = 384
SLAB = 2 * BLK
ROWS = 64
PATCH = 256
CAP = 1024
UNIT = 32
UNITS = PATCH // UNIT
UNIT1 = 32
UNITS1 = PATCH // UNIT1
AT_ONCE = 5
CHUNK = 128
TOTAL = 960
WIDTH = 3072
HALF = WIDTH // 2
EXP2_SCALE = math.log2(math.e) / math.sqrt(HD)


def mult(value, of):
    return pl.multiple_of(value, of)


def kernel(
    n_pipe,
    x_hbm,
    k_hbm,
    v_hbm,
    w_hbm,
    shift_hbm,
    scale_hbm,
    gate_hbm,
    qg_hbm,
    kg_hbm,
    lengths_hbm,
    first_patch,
    out_ref,
    xv,
    kv,
    vv,
    w4,
    shv,
    scv,
    gav,
    qgv,
    kgv,
    md,
    res,
    qb,
    fh,
    att1,
    sb1,
    rb1,
    fw1,
    xs,
    st2,
    om,
    ml,
    rx,
    as2,
    att2,
    sb2,
    rb2,
    fw2,
    lengths,
    lsem,
    md_s,
    md_r,
    res_s,
    res_r,
    w_s,
    w_r,
    a1_s,
    a1_r,
    p1_s,
    p1_r,
    f1_s,
    f1_r,
    s2_s,
    s2_r,
    rx_s,
    rx_r,
    a2_s,
    a2_r,
    p2_s,
    p2_r,
    f2_s,
    f2_r,
):
    s = lax.axis_index("pipe")
    q = lax.axis_index("seq")
    j = q // 2
    c = q % 2
    odd = s % 2
    even = odd == 0
    pair = s + 1 - 2 * odd
    ahead = (s + 2) % n_pipe
    behind = (s + n_pipe - 2) % n_pipe
    chip = [j, 1 - j]
    slab = [2 * chip[0] + c, 2 * chip[1] + c]
    mate_slab = [2 * chip[0] + (1 - c), 2 * chip[1] + (1 - c)]
    peer = {1: mate_slab[0], 2: slab[1], 3: mate_slab[1]}
    mate = peer[1]
    own_rows = pl.ds(mult(ROWS * q, ROWS), ROWS)
    own_cols = pl.ds(mult(BLK * c, BLK), BLK)
    lane = lax.broadcasted_iota(jnp.int32, (ROWS, 128), 1)
    sub = lax.broadcasted_iota(jnp.int32, (ROWS, 128), 0)

    def block_cols(g, e):
        return pl.ds(mult(HALF * e + BLK * g, 128), BLK)

    def remote(src, dst, ssem, rsem, pipe, seq):
        return pltpu.make_async_remote_copy(
            src_ref=src,
            dst_ref=dst,
            send_sem=ssem,
            recv_sem=rsem,
            device_id={"pipe": pipe, "seq": seq},
            device_id_type=MESH,
        )

    bar = pltpu.get_barrier_semaphore()
    for k in (1, 2, 3):
        pl.semaphore_signal(bar, inc=1, device_id={"pipe": s, "seq": peer[k]}, device_id_type=MESH)
    for v in (0, 1):
        pl.semaphore_signal(bar, inc=1, device_id={"pipe": pair, "seq": slab[v]}, device_id_type=MESH)
    pl.semaphore_signal(bar, inc=1, device_id={"pipe": behind, "seq": q}, device_id_type=MESH)

    local = []

    def load(src, dst):
        copy = pltpu.make_async_copy(src, dst, lsem.at[len(local)])
        copy.start()
        local.append(copy)
        return copy

    ld_x = load(x_hbm, xv)
    ld_sc = load(scale_hbm, scv)
    ld_sh = load(shift_hbm, shv)
    ld_small = [load(gate_hbm, gav), load(qg_hbm, qgv), load(kg_hbm, kgv), load(lengths_hbm, lengths)]
    ld_k = load(k_hbm.at[0], kv)
    ld_v = load(v_hbm.at[0], vv)

    ld_x.wait()
    xf = xv[...].astype(F32)
    mean = jnp.sum(xf, axis=1, keepdims=True) * (1.0 / WIDTH)
    cent = xf - mean
    var = jnp.sum(cent * cent, axis=1, keepdims=True) * (1.0 / WIDTH)
    rstd = lax.rsqrt(var + EPS)
    ld_sc.wait()
    ld_sh.wait()
    md[...] = (
        (xv[:, :HALF].astype(F32) - mean) * rstd * (1.0 + scv[:, :HALF]) + shv[:, :HALF]
    ).astype(BF16)
    fh[own_rows, BLK:] = md[:, pl.ds(mult(BLK * q, 128), BLK)]

    for copy in ld_small:
        copy.wait()
    head_cols = pl.ds(mult(BLK * q, 128), BLK)
    scale_h = 1.0 + scv[:, head_cols]
    shift_h = shv[:, head_cols]
    q_gain = qgv[...]
    k_gain = kgv[...]

    def heads(modded, rows):
        mf = modded.astype(F32)
        for h in range(BLK // HD):
            part = mf[:, HD * h : HD * (h + 1)]
            normed = part * lax.rsqrt(jnp.sum(part * part, axis=1, keepdims=True) * (1.0 / HD) + EPS)
            qb[rows, HD * h : HD * (h + 1)] = (normed * q_gain).astype(BF16)
            fh[rows, HD * h : HD * (h + 1)] = (normed * k_gain).astype(BF16)

    pl.semaphore_wait(bar, 6)

    md_copies = {}
    for k in (2, 3, 1):
        md_copies[k] = remote(
            md.at[:, pl.ds(mult(BLK * peer[k], 128), BLK)],
            fh.at[own_rows, pl.ds(BLK, BLK)],
            md_s.at[k - 1],
            md_r.at[k - 1],
            s,
            peer[k],
        )
        md_copies[k].start()

    ld_res = []
    res_copies = []
    for v in (0, 1):
        for e in (0, 1):
            dst = res.at[v, pl.ds(mult(ROWS * c, ROWS), ROWS), pl.ds(BLK * e, BLK)]
            ld_res.append(load(x_hbm.at[:, block_cols(slab[v], e)], dst))
            copy = remote(
                x_hbm.at[:, block_cols(mate_slab[v], e)], dst, res_s.at[2 * v + e], res_r.at[2 * v + e], s, mate
            )
            copy.start()
            res_copies.append(copy)

    ld_w = []
    w_copies = []
    for n, (mine, his) in enumerate(
        [(slab[0], mate_slab[0]), (slab[1], mate_slab[1]), (mate_slab[0], slab[0]), (mate_slab[1], slab[1])]
    ):
        for e in (0, 1):
            for g, away in ((mine, False), (his, True)):
                src = w_hbm.at[0, :, block_cols(g, e)]
                dst = w4.at[g, own_cols, pl.ds(BLK * e, BLK)]
                if away:
                    copy = remote(src, dst, w_s.at[2 * n + e], w_r.at[2 * n + e], s, mate)
                    copy.start()
                    w_copies.append(copy)
                else:
                    ld_w.append(load(src, dst))

    def patch_at(t):
        p = (first_patch[0] + t + n_pipe * NP - s) % NP
        first = jnp.int32(0)
        length = jnp.int32(0)
        for n in range(NP):
            first = first + jnp.where(n < p, lengths[n], 0)
            length = length + jnp.where(n == p, lengths[n], 0)
        return first, length

    def refresh(first, length):
        def block(n, carry):
            rows = pl.ds(mult(n * PATCH, PATCH), PATCH)
            row = lax.broadcasted_iota(jnp.int32, (PATCH, PATCH), 0) + n * PATCH
            col = lax.broadcasted_iota(jnp.int32, (PATCH, PATCH), 1)
            pick = jnp.where((row - first == col) & (col < length), 1.0, 0.0).astype(BF16)
            placed = jnp.dot(pick, fh[...], preferred_element_type=F32)
            at = lax.broadcasted_iota(jnp.int32, (PATCH, BLK), 0) + n * PATCH
            inside = (at >= first) & (at < first + length)
            kv[rows, :] = jnp.where(inside, placed[:, :BLK], kv[rows, :].astype(F32)).astype(BF16)
            vv[rows, :] = jnp.where(inside, placed[:, BLK:], vv[rows, :].astype(F32)).astype(BF16)
            return carry

        lax.fori_loop(0, CAP // PATCH, block, 0)

    def stale_bias(first, length):
        at = lax.broadcasted_iota(jnp.int32, (1, CAP), 1)
        gone = ((at >= first) & (at < first + length)) | (at >= TOTAL)
        return jnp.where(gone, MASKED, 0.0)

    def stale_scores(queries, h, bias):
        cols = slice(HD * h, HD * (h + 1))
        return bias + lax.dot_general(
            queries[:, cols], kv[:, cols], (((1,), (1,)), ((), ())), preferred_element_type=F32
        )

    def fresh_scores(queries, h, length):
        cols = slice(HD * h, HD * (h + 1))
        scores = lax.dot_general(
            queries[:, cols], fh[:, cols], (((1,), (1,)), ((), ())), preferred_element_type=F32
        )
        at = lax.broadcasted_iota(jnp.int32, scores.shape, 1)
        return jnp.where(at < length, scores, MASKED)

    def weigh(scores, top):
        weight = jnp.exp2((scores - top) * EXP2_SCALE)
        return weight.astype(BF16), jnp.sum(weight, axis=1, keepdims=True)

    def stale_values(weight, h):
        return jnp.dot(weight, vv[:, HD * h : HD * (h + 1)], preferred_element_type=F32)

    def fresh_values(weight, h):
        cols = slice(BLK + HD * h, BLK + HD * (h + 1))
        return jnp.dot(weight, fh[:, cols], preferred_element_type=F32)

    heads_here = range(BLK // HD)

    def tops(scores):
        return [jnp.max(part, axis=1, keepdims=True) for part in scores]

    def attend(queries, live, bias, length):
        old = [stale_scores(queries, h, bias) for h in heads_here]
        new = [fresh_scores(queries, h, length) for h in heads_here]
        top = [jnp.maximum(a, b) for a, b in zip(tops(old), tops(new))]
        old = [weigh(part, m) for part, m in zip(old, top)]
        new = [weigh(part, m) for part, m in zip(new, top)]
        out = [stale_values(old[h][0], h) + fresh_values(new[h][0], h) for h in heads_here]
        return jnp.concatenate(
            [jnp.where(live, out[h] / (old[h][1] + new[h][1]), 0.0).astype(BF16) for h in heads_here], axis=1
        )

    def soften(scores, values):
        top = tops(scores)
        weight = [weigh(part, m) for part, m in zip(scores, top)]
        return top, [part[1] for part in weight], [values(weight[h][0], h) for h in heads_here]

    def keep_stale(rows, top, total, out):
        tile = jnp.zeros((ROWS, 128), F32)
        for h in heads_here:
            tile = jnp.where(lane == h, top[h], jnp.where(lane == 8 + h, total[h], tile))
        om[rows, :] = jnp.concatenate(out, axis=1)
        ml[rows, :] = tile

    def attend_stale(rows, bias):
        queries = qb[rows, :]
        keep_stale(rows, *soften([stale_scores(queries, h, bias) for h in heads_here], stale_values))

    def merge_parts(out, tile, fresh, live):
        parts = []
        for h, (top, total, got) in enumerate(zip(*fresh)):
            old_top, old_total = tile[:, h : h + 1], tile[:, 8 + h : 9 + h]
            both = jnp.maximum(old_top, top)
            a = jnp.exp2((old_top - both) * EXP2_SCALE)
            b = jnp.exp2((top - both) * EXP2_SCALE)
            got = out[:, HD * h : HD * (h + 1)] * a + got * b
            parts.append(jnp.where(live, got / (old_total * a + total * b), 0.0).astype(BF16))
        return jnp.concatenate(parts, axis=1)

    def gates(g):
        lo = gav[:, pl.ds(mult(BLK * g, 128), BLK)]
        hi = gav[:, pl.ds(mult(HALF + BLK * g, 128), BLK)]
        return jnp.concatenate([lo, hi], axis=1)

    first, length = patch_at(0)
    heads(fh[own_rows, BLK:], own_rows)
    for k in (1, 2, 3):
        md_copies[k].wait_recv()
        rows = pl.ds(mult(ROWS * peer[k], ROWS), ROWS)
        heads(fh[rows, BLK:], rows)
    ld_k.wait()
    ld_v.wait()
    bias = stale_bias(first, length)
    next_first, next_length = patch_at(1)
    next_bias = stale_bias(next_first, next_length)

    def unit_rows(i):
        return pl.ds(mult(i * UNIT, UNIT), UNIT)

    def unit1_rows(i):
        return pl.ds(mult(i * UNIT1, UNIT1), UNIT1)

    def att1_copy(i):
        part = att1.at[pl.ds(mult(i * CHUNK, CHUNK), CHUNK), own_cols]
        return remote(part, part, a1_s.at[i], a1_r.at[i], s, mate)

    def p1_copy(i, v):
        rows = unit1_rows(i)
        return remote(sb1.at[v, rows], rb1.at[v, rows], p1_s.at[v, i], p1_r.at[v, i], pair, slab[v])

    def f1_copy(i):
        rows = unit1_rows(i)
        return remote(fw1.at[rows], xs.at[rows], f1_s.at[i], f1_r.at[i], ahead, q)

    for copy in ld_res:
        copy.wait()
    for copy in res_copies:
        copy.wait_recv()
    for copy in ld_w[:4]:
        copy.wait()
    for copy in w_copies[:4]:
        copy.wait_recv()

    gate1 = [gates(slab[0]), gates(slab[1])]

    def s2_copy(g, k):
        return remote(st2.at[0, g], st2.at[k, g], s2_s.at[k - 1, g], s2_r.at[k - 1, g], s, peer[k])

    def rx_copy(g):
        v = jnp.where(g // 2 == j, 0, 1)
        src = xs.at[pl.ds(mult(g * ROWS, ROWS), ROWS)]
        return remote(src, rx.at[v], rx_s.at[v], rx_r.at[v], s, mate)

    def ready(g):
        hf = xs[pl.ds(mult(g * ROWS, ROWS), ROWS), :].astype(F32)
        mean = jnp.sum(hf, axis=1, keepdims=True) * (1.0 / SLAB)
        cent = hf - mean
        spread = jnp.sum(cent * cent, axis=1, keepdims=True)
        tile = jnp.where(lane == sub, mean, jnp.where(lane == sub + ROWS, spread, 0.0))
        st2[0, g] = jnp.sum(tile, axis=0, keepdims=True)
        for k in (2, 3, 1):
            s2_copy(g, k).start()

        @pl.when(g % 2 != c)
        def _():
            rx_copy(g).start()

    def process(g):
        for k in (1, 2, 3):
            s2_copy(g, k).wait_recv()
        stats = [st2[k, g] for k in range(4)]
        total = stats[0] + stats[1] + stats[2] + stats[3]
        means = total * 0.25
        apart = jnp.zeros((1, 128), F32)
        for stat in stats:
            apart = apart + (stat - means) * (stat - means) * SLAB
        both = jnp.where(lane[:1] < ROWS, apart, total)
        mean = jnp.sum(jnp.where(lane == sub, means, 0.0), axis=1, keepdims=True)
        spread = jnp.sum(
            jnp.where((lane == sub) | (lane == sub + ROWS), both, 0.0), axis=1, keepdims=True
        )
        rstd = lax.rsqrt(spread * (1.0 / WIDTH) + EPS)
        rows = pl.ds(mult(g * ROWS, ROWS), ROWS)
        modded = ((xs[rows, :BLK].astype(F32) - mean) * rstd * scale_h + shift_h).astype(BF16)
        fh[rows, BLK:] = modded
        heads(modded, rows)

        @pl.when(g < groups - 1)
        def _():
            attend_stale(rows, next_bias)

    def take(g):
        for u in range(ROWS // UNIT1):
            i = g * (ROWS // UNIT1) + u
            for v in (0, 1):
                p1_copy(i, v).wait_recv()
            rows = unit1_rows(i)
            held = (rb1[0, rows, :].astype(F32) + rb1[1, rows, :].astype(F32)).astype(BF16)

            @pl.when(even)
            def _():
                fw1[rows, :] = held
                f1_copy(i).start()

            @pl.when(jnp.logical_not(even))
            def _():
                xs[rows, :] = held

    def taken(g):
        for u in range(ROWS // UNIT1):
            f1_copy(g * (ROWS // UNIT1) + u).wait_recv()

    groups = PATCH // ROWS

    def step0(i, carry):
        rows = pl.ds(mult(i * CHUNK, CHUNK), CHUNK)
        live = lax.broadcasted_iota(jnp.int32, (CHUNK, HD), 0) + i * CHUNK < length
        att1[rows, own_cols] = attend(qb[rows, :], live, bias, length)
        att1_copy(i).start()
        att1_copy(i).wait_recv()
        live = lax.broadcasted_iota(jnp.int32, (CHUNK, SLAB), 0) + i * CHUNK < length
        keep = live & (i == j)
        for v in (0, 1):
            proj = jnp.dot(att1[rows, :], w4[slab[v]], preferred_element_type=F32)
            held = res[v].astype(F32)
            sb1[v, rows, :] = (proj * gate1[v] + jnp.where(keep, held, 0.0)).astype(BF16)
            for u in range(CHUNK // UNIT1):

                @pl.when(i * (CHUNK // UNIT1) + u < AT_ONCE)
                def _():
                    p1_copy(i * (CHUNK // UNIT1) + u, v).start()

        return carry

    lax.fori_loop(0, PATCH // CHUNK, step0, 0)
    refresh(first, length)

    def hand_over(i, carry):
        @pl.when(i < groups)
        def _():
            take(i)

        @pl.when((i < groups) & jnp.logical_not(even))
        def _():
            ready(i)

        @pl.when((i >= 1) & (i < 1 + groups) & even)
        def _():
            taken(i - 1)
            ready(i - 1)

        for u in range(AT_ONCE, UNITS1):

            @pl.when(i == (u - AT_ONCE) // 2)
            def _():
                for v in (0, 1):
                    p1_copy(u, v).start()

        done = i - 1 - (1 - odd)

        @pl.when((done >= 0) & (done < groups))
        def _():
            process(done)

        return carry

    lax.fori_loop(0, groups + 2, hand_over, 0)

    first, length = next_first, next_length

    def att2_copy(i):
        rows = pl.ds(mult(i * ROWS, ROWS), ROWS)
        return remote(as2.at[rows], att2.at[rows, own_cols], a2_s.at[i], a2_r.at[i], s, mate)

    def slab_of(u):
        p = u % 4
        return 2 * (p // 2) + (c + p % 2) % 2

    def p2_copy(u, e, v):
        return remote(sb2.at[v, u, e], rb2.at[v, u, e], p2_s.at[v, u, e], p2_r.at[v, u, e], pair, slab[v])

    def f2_copy(u, e):
        dst = out_ref.at[unit_rows(u // 4), block_cols(slab_of(u), e)]
        return remote(fw2.at[u, e], dst, f2_s.at[u, e], f2_r.at[u, e], ahead, q)

    for v in (0, 1):
        rx_copy(mate_slab[v]).wait_recv()
    for copy in ld_w[4:]:
        copy.wait()
    for copy in w_copies[4:]:
        copy.wait_recv()

    bases = [ROWS * slab[0], ROWS * slab[1], ROWS * mate_slab[0], ROWS * mate_slab[1]]

    def finish(u):
        for e in (0, 1):
            for v in (0, 1):
                p2_copy(u, e, v).wait_recv()
            held = (rb2[0, u, e].astype(F32) + rb2[1, u, e].astype(F32)).astype(BF16)

            @pl.when(even)
            def _():
                fw2[u, e] = held
                f2_copy(u, e).start()

            @pl.when(jnp.logical_not(even))
            def _():
                out_ref[unit_rows(u // 4), block_cols(slab_of(u), e)] = held

    r = lax.broadcasted_iota(jnp.int32, (4 * UNIT, HD), 0)
    seg = r // UNIT
    start = jnp.where(
        seg == 0, bases[0], jnp.where(seg == 1, bases[1], jnp.where(seg == 2, bases[2], bases[3]))
    )

    def merge(i, last=None):
        seen = [pl.ds(mult(base + UNIT * i, UNIT), UNIT) for base in bases]
        queries = jnp.concatenate([qb[part, :] for part in seen], axis=0)
        new = [fresh_scores(queries, h, length) for h in heads_here]
        if last is None:
            fresh = soften(new, fresh_values)
        else:
            late = qb[last, :]
            old = [stale_scores(late, h, next_bias) for h in heads_here]
            old_top, new_top = tops(old), tops(new)
            old = [weigh(part, m) for part, m in zip(old, old_top)]
            new = [weigh(part, m) for part, m in zip(new, new_top)]
            old_out = [stale_values(old[h][0], h) for h in heads_here]
            fresh = new_top, [part[1] for part in new], [fresh_values(new[h][0], h) for h in heads_here]
            keep_stale(last, old_top, [part[1] for part in old], old_out)
        out = jnp.concatenate([om[part, :] for part in seen], axis=0)
        tile = jnp.concatenate([ml[part, :] for part in seen], axis=0)
        live = start + UNIT * i + r % UNIT < length
        got = merge_parts(out, tile, fresh, live)
        rows = pl.ds(i * ROWS, ROWS)
        att2[rows, own_cols] = got[:ROWS]
        as2[rows, :] = got[ROWS:]
        att2_copy(i).start()

    merge(0, pl.ds(PATCH - ROWS, ROWS))
    merge(1)

    def step1(u, carry):
        n = u // 4
        p = u % 4

        @pl.when(p == 0)
        def _():
            att2_copy(n).wait_recv()

        g = slab_of(u)
        part = unit_rows(n)
        left = att2[pl.ds(mult(n * ROWS, ROWS), ROWS), :]
        proj = jnp.dot(left, w4[g], preferred_element_type=F32) * gates(g)
        own = jnp.concatenate(
            [xs[pl.ds(mult(base + UNIT * n, UNIT), UNIT), :] for base in bases[:2]], axis=0
        )
        his = jnp.concatenate([rx[0, part, :], rx[1, part, :]], axis=0)
        held = jnp.where(p % 2 == 0, own.astype(F32), his.astype(F32))
        proj = (proj + jnp.where(p // 2 == j, held, 0.0)).astype(BF16)
        for v in (0, 1):
            for e in (0, 1):
                sb2[v, u, e] = proj[v * UNIT : (v + 1) * UNIT, e * BLK : (e + 1) * BLK]
                p2_copy(u, e, v).start()

        @pl.when(even)
        def _():
            finish(u)

        return carry

    lax.fori_loop(0, UNITS, step1, 0)

    @pl.when(jnp.logical_not(even))
    def _():
        def rest(u, carry):
            finish(u)
            return carry

        lax.fori_loop(0, UNITS, rest, 0)

    @pl.when(even)
    def _():
        for i in range(UNITS1):
            f1_copy(i).wait_send()
        for u in range(UNITS):
            for e in (0, 1):
                f2_copy(u, e).wait()

    for k in (1, 2, 3):
        md_copies[k].wait_send()
        for g in range(groups):
            s2_copy(g, k).wait_send()
    for v in (0, 1):
        rx_copy(mate_slab[v]).wait_send()
    for copy in res_copies + w_copies:
        copy.wait_send()
    for i in range(PATCH // CHUNK):
        att1_copy(i).wait_send()
    for i in range(UNITS1):
        for v in (0, 1):
            p1_copy(i, v).wait_send()
    for u in range(UNITS):
        for v in (0, 1):
            for e in (0, 1):
                p2_copy(u, e, v).wait_send()
    for i in range(2):
        att2_copy(i).wait_send()


def shards(n_pipe, *args):
    dma = pltpu.SemaphoreType.DMA
    vmem = pltpu.VMEM
    any_space = pl.BlockSpec(memory_space=pl.ANY)
    smem = pl.BlockSpec(memory_space=pltpu.SMEM)
    chunks = PATCH // ROWS
    held = [pltpu.with_memory_space_constraint(arg, pltpu.HBM) for arg in args[:10]]
    return pl.pallas_call(
        functools.partial(kernel, n_pipe),
        out_shape=jax.ShapeDtypeStruct((ROWS, WIDTH), BF16),
        in_specs=[any_space] * 10 + [smem],
        out_specs=pl.BlockSpec(memory_space=vmem),
        scratch_shapes=[
            vmem((ROWS, WIDTH), BF16),
            vmem((CAP, BLK), BF16),
            vmem((CAP, BLK), BF16),
            vmem((4, SLAB, SLAB), BF16),
            vmem((1, WIDTH), F32),
            vmem((1, WIDTH), F32),
            vmem((1, WIDTH), F32),
            vmem((1, HD), F32),
            vmem((1, HD), F32),
            vmem((ROWS, HALF), BF16),
            vmem((2, 2 * ROWS, SLAB), BF16),
            vmem((PATCH, BLK), BF16),
            vmem((PATCH, SLAB), BF16),
            vmem((PATCH, SLAB), BF16),
            vmem((2, PATCH, SLAB), BF16),
            vmem((2, PATCH, SLAB), BF16),
            vmem((PATCH, SLAB), BF16),
            vmem((PATCH, SLAB), BF16),
            vmem((4, chunks, 1, 128), F32),
            vmem((PATCH, BLK), F32),
            vmem((PATCH, 128), F32),
            vmem((2, ROWS, SLAB), BF16),
            vmem((2 * ROWS, BLK), BF16),
            vmem((2 * ROWS, SLAB), BF16),
            vmem((2, UNITS, 2, UNIT, BLK), BF16),
            vmem((2, UNITS, 2, UNIT, BLK), BF16),
            vmem((UNITS, 2, UNIT, BLK), BF16),
            pltpu.SMEM((NP,), jnp.int32),
            dma((21,)),
            dma((3,)),
            dma((3,)),
            dma((4,)),
            dma((4,)),
            dma((8,)),
            dma((8,)),
            dma((PATCH // CHUNK,)),
            dma((PATCH // CHUNK,)),
            dma((2, UNITS1)),
            dma((2, UNITS1)),
            dma((UNITS1,)),
            dma((UNITS1,)),
            dma((3, chunks)),
            dma((3, chunks)),
            dma((2,)),
            dma((2,)),
            dma((2,)),
            dma((2,)),
            dma((2, UNITS, 2)),
            dma((2, UNITS, 2)),
            dma((UNITS, 2)),
            dma((UNITS, 2)),
        ],
        compiler_params=pltpu.CompilerParams(
            collective_id=0, has_side_effects=True, vmem_limit_bytes=40 << 20
        ),
        name="section_steps",
    )(*held, args[10])


def solution(mesh):
    in_specs = (
        P(("pipe", "seq"), None),
        P("pipe", None, "seq"),
        P("pipe", None, "seq"),
        P("pipe", "seq", None),
        P("pipe", None),
        P("pipe", None),
        P("pipe", None),
        P("pipe", None),
        P("pipe", None),
        P(),
        P(),
    )
    return jax.shard_map(
        functools.partial(shards, mesh.shape["pipe"]),
        mesh=mesh,
        in_specs=in_specs,
        out_specs=P(("pipe", "seq"), None),
        check_vma=False,
    )
```

```python
import functools
import math

import jax
import jax.numpy as jnp
from jax import lax
from jax.experimental import pallas as pl
from jax.experimental.pallas import tpu as pltpu
from jax.sharding import PartitionSpec as P

MESH = pl.DeviceIdType.MESH
BF16 = jnp.bfloat16
F32 = jnp.float32

NP = 4
EPS = 1e-06
MASKED = -1e30
HD = 128
BLK = 384
SLAB = 2 * BLK
ROWS = 64
PATCH = 256
CAP = 1024
UNIT = 32
UNITS = PATCH // UNIT
UNIT1 = 32
UNITS1 = PATCH // UNIT1
AT_ONCE = 5
CHUNK = 128
TOTAL = 960
WIDTH = 3072
HALF = WIDTH // 2
EXP2_SCALE = math.log2(math.e) / math.sqrt(HD)


def mult(value, of):
    return pl.multiple_of(value, of)


def kernel(
    n_pipe,
    x_hbm,
    k_hbm,
    v_hbm,
    w_hbm,
    shift_hbm,
    scale_hbm,
    gate_hbm,
    qg_hbm,
    kg_hbm,
    lengths_hbm,
    first_patch,
    out_ref,
    xv,
    kv,
    vv,
    w4,
    shv,
    scv,
    gav,
    qgv,
    kgv,
    md,
    res,
    qb,
    fh,
    att1,
    sb1,
    rb1,
    fw1,
    xs,
    st2,
    om,
    ml,
    rx,
    as2,
    att2,
    sb2,
    rb2,
    fw2,
    lengths,
    lsem,
    md_s,
    md_r,
    res_s,
    res_r,
    w_s,
    w_r,
    a1_s,
    a1_r,
    p1_s,
    p1_r,
    f1_s,
    f1_r,
    s2_s,
    s2_r,
    rx_s,
    rx_r,
    a2_s,
    a2_r,
    p2_s,
    p2_r,
    f2_s,
    f2_r,
):
    s = lax.axis_index("pipe")
    q = lax.axis_index("seq")
    j = q // 2
    c = q % 2
    odd = s % 2
    even = odd == 0
    pair = s + 1 - 2 * odd
    ahead = (s + 2) % n_pipe
    behind = (s + n_pipe - 2) % n_pipe
    chip = [j, 1 - j]
    slab = [2 * chip[0] + c, 2 * chip[1] + c]
    mate_slab = [2 * chip[0] + (1 - c), 2 * chip[1] + (1 - c)]
    peer = {1: mate_slab[0], 2: slab[1], 3: mate_slab[1]}
    mate = peer[1]
    own_rows = pl.ds(mult(ROWS * q, ROWS), ROWS)
    own_cols = pl.ds(mult(BLK * c, BLK), BLK)
    lane = lax.broadcasted_iota(jnp.int32, (ROWS, 128), 1)
    sub = lax.broadcasted_iota(jnp.int32, (ROWS, 128), 0)

    def block_cols(g, e):
        return pl.ds(mult(HALF * e + BLK * g, 128), BLK)

    def remote(src, dst, ssem, rsem, pipe, seq):
        return pltpu.make_async_remote_copy(
            src_ref=src,
            dst_ref=dst,
            send_sem=ssem,
            recv_sem=rsem,
            device_id={"pipe": pipe, "seq": seq},
            device_id_type=MESH,
        )

    bar = pltpu.get_barrier_semaphore()
    for k in (1, 2, 3):
        pl.semaphore_signal(bar, inc=1, device_id={"pipe": s, "seq": peer[k]}, device_id_type=MESH)
    for v in (0, 1):
        pl.semaphore_signal(bar, inc=1, device_id={"pipe": pair, "seq": slab[v]}, device_id_type=MESH)
    pl.semaphore_signal(bar, inc=1, device_id={"pipe": behind, "seq": q}, device_id_type=MESH)

    local = []

    def load(src, dst):
        copy = pltpu.make_async_copy(src, dst, lsem.at[len(local)])
        copy.start()
        local.append(copy)
        return copy

    ld_x = load(x_hbm, xv)
    ld_sc = load(scale_hbm, scv)
    ld_sh = load(shift_hbm, shv)
    ld_small = [load(gate_hbm, gav), load(qg_hbm, qgv), load(kg_hbm, kgv), load(lengths_hbm, lengths)]
    ld_k = load(k_hbm.at[0], kv)
    ld_v = load(v_hbm.at[0], vv)

    ld_x.wait()
    xf = xv[...].astype(F32)
    mean = jnp.sum(xf, axis=1, keepdims=True) * (1.0 / WIDTH)
    cent = xf - mean
    var = jnp.sum(cent * cent, axis=1, keepdims=True) * (1.0 / WIDTH)
    rstd = lax.rsqrt(var + EPS)
    ld_sc.wait()
    ld_sh.wait()
    md[...] = (
        (xv[:, :HALF].astype(F32) - mean) * rstd * (1.0 + scv[:, :HALF]) + shv[:, :HALF]
    ).astype(BF16)
    fh[own_rows, BLK:] = md[:, pl.ds(mult(BLK * q, 128), BLK)]

    for copy in ld_small:
        copy.wait()
    head_cols = pl.ds(mult(BLK * q, 128), BLK)
    scale_h = 1.0 + scv[:, head_cols]
    shift_h = shv[:, head_cols]
    q_gain = qgv[...]
    k_gain = kgv[...]

    def heads(modded, rows):
        mf = modded.astype(F32)
        for h in range(BLK // HD):
            part = mf[:, HD * h : HD * (h + 1)]
            normed = part * lax.rsqrt(jnp.sum(part * part, axis=1, keepdims=True) * (1.0 / HD) + EPS)
            qb[rows, HD * h : HD * (h + 1)] = (normed * q_gain).astype(BF16)
            fh[rows, HD * h : HD * (h + 1)] = (normed * k_gain).astype(BF16)

    pl.semaphore_wait(bar, 6)

    md_copies = {}
    for k in (2, 3, 1):
        md_copies[k] = remote(
            md.at[:, pl.ds(mult(BLK * peer[k], 128), BLK)],
            fh.at[own_rows, pl.ds(BLK, BLK)],
            md_s.at[k - 1],
            md_r.at[k - 1],
            s,
            peer[k],
        )
        md_copies[k].start()

    ld_res = []
    res_copies = []
    for v in (0, 1):
        for e in (0, 1):
            dst = res.at[v, pl.ds(mult(ROWS * c, ROWS), ROWS), pl.ds(BLK * e, BLK)]
            ld_res.append(load(x_hbm.at[:, block_cols(slab[v], e)], dst))
            copy = remote(
                x_hbm.at[:, block_cols(mate_slab[v], e)], dst, res_s.at[2 * v + e], res_r.at[2 * v + e], s, mate
            )
            copy.start()
            res_copies.append(copy)

    ld_w = []
    w_copies = []
    for n, (mine, his) in enumerate(
        [(slab[0], mate_slab[0]), (slab[1], mate_slab[1]), (mate_slab[0], slab[0]), (mate_slab[1], slab[1])]
    ):
        for e in (0, 1):
            for g, away in ((mine, False), (his, True)):
                src = w_hbm.at[0, :, block_cols(g, e)]
                dst = w4.at[g, own_cols, pl.ds(BLK * e, BLK)]
                if away:
                    copy = remote(src, dst, w_s.at[2 * n + e], w_r.at[2 * n + e], s, mate)
                    copy.start()
                    w_copies.append(copy)
                else:
                    ld_w.append(load(src, dst))

    def patch_at(t):
        p = (first_patch[0] + t + n_pipe * NP - s) % NP
        first = jnp.int32(0)
        length = jnp.int32(0)
        for n in range(NP):
            first = first + jnp.where(n < p, lengths[n], 0)
            length = length + jnp.where(n == p, lengths[n], 0)
        return first, length

    def refresh(first, length):
        def block(n, carry):
            rows = pl.ds(mult(n * PATCH, PATCH), PATCH)
            row = lax.broadcasted_iota(jnp.int32, (PATCH, PATCH), 0) + n * PATCH
            col = lax.broadcasted_iota(jnp.int32, (PATCH, PATCH), 1)
            pick = jnp.where((row - first == col) & (col < length), 1.0, 0.0).astype(BF16)
            placed = jnp.dot(pick, fh[...], preferred_element_type=F32)
            at = lax.broadcasted_iota(jnp.int32, (PATCH, BLK), 0) + n * PATCH
            inside = (at >= first) & (at < first + length)
            kv[rows, :] = jnp.where(inside, placed[:, :BLK], kv[rows, :].astype(F32)).astype(BF16)
            vv[rows, :] = jnp.where(inside, placed[:, BLK:], vv[rows, :].astype(F32)).astype(BF16)
            return carry

        lax.fori_loop(0, CAP // PATCH, block, 0)

    def stale_bias(first, length):
        at = lax.broadcasted_iota(jnp.int32, (1, CAP), 1)
        gone = ((at >= first) & (at < first + length)) | (at >= TOTAL)
        return jnp.where(gone, MASKED, 0.0)

    def stale_scores(queries, h, bias):
        cols = slice(HD * h, HD * (h + 1))
        return bias + lax.dot_general(
            queries[:, cols], kv[:, cols], (((1,), (1,)), ((), ())), preferred_element_type=F32
        )

    def fresh_scores(queries, h, length):
        cols = slice(HD * h, HD * (h + 1))
        scores = lax.dot_general(
            queries[:, cols], fh[:, cols], (((1,), (1,)), ((), ())), preferred_element_type=F32
        )
        at = lax.broadcasted_iota(jnp.int32, scores.shape, 1)
        return jnp.where(at < length, scores, MASKED)

    def weigh(scores, top):
        weight = jnp.exp2((scores - top) * EXP2_SCALE)
        return weight.astype(BF16), jnp.sum(weight, axis=1, keepdims=True)

    def stale_values(weight, h):
        return jnp.dot(weight, vv[:, HD * h : HD * (h + 1)], preferred_element_type=F32)

    def fresh_values(weight, h):
        cols = slice(BLK + HD * h, BLK + HD * (h + 1))
        return jnp.dot(weight, fh[:, cols], preferred_element_type=F32)

    heads_here = range(BLK // HD)

    def tops(scores):
        return [jnp.max(part, axis=1, keepdims=True) for part in scores]

    def attend(queries, live, bias, length):
        old = [stale_scores(queries, h, bias) for h in heads_here]
        new = [fresh_scores(queries, h, length) for h in heads_here]
        top = [jnp.maximum(a, b) for a, b in zip(tops(old), tops(new))]
        old = [weigh(part, m) for part, m in zip(old, top)]
        new = [weigh(part, m) for part, m in zip(new, top)]
        out = [stale_values(old[h][0], h) + fresh_values(new[h][0], h) for h in heads_here]
        return jnp.concatenate(
            [jnp.where(live, out[h] / (old[h][1] + new[h][1]), 0.0).astype(BF16) for h in heads_here], axis=1
        )

    def soften(scores, values):
        top = tops(scores)
        weight = [weigh(part, m) for part, m in zip(scores, top)]
        return top, [part[1] for part in weight], [values(weight[h][0], h) for h in heads_here]

    def keep_stale(rows, top, total, out):
        tile = jnp.zeros((ROWS, 128), F32)
        for h in heads_here:
            tile = jnp.where(lane == h, top[h], jnp.where(lane == 8 + h, total[h], tile))
        om[rows, :] = jnp.concatenate(out, axis=1)
        ml[rows, :] = tile

    def attend_stale(rows, bias):
        queries = qb[rows, :]
        keep_stale(rows, *soften([stale_scores(queries, h, bias) for h in heads_here], stale_values))

    def merge_parts(out, tile, fresh, live):
        parts = []
        for h, (top, total, got) in enumerate(zip(*fresh)):
            old_top, old_total = tile[:, h : h + 1], tile[:, 8 + h : 9 + h]
            both = jnp.maximum(old_top, top)
            a = jnp.exp2((old_top - both) * EXP2_SCALE)
            b = jnp.exp2((top - both) * EXP2_SCALE)
            got = out[:, HD * h : HD * (h + 1)] * a + got * b
            parts.append(jnp.where(live, got / (old_total * a + total * b), 0.0).astype(BF16))
        return jnp.concatenate(parts, axis=1)

    def gates(g):
        lo = gav[:, pl.ds(mult(BLK * g, 128), BLK)]
        hi = gav[:, pl.ds(mult(HALF + BLK * g, 128), BLK)]
        return jnp.concatenate([lo, hi], axis=1)

    first, length = patch_at(0)
    heads(fh[own_rows, BLK:], own_rows)
    for k in (1, 2, 3):
        md_copies[k].wait_recv()
        rows = pl.ds(mult(ROWS * peer[k], ROWS), ROWS)
        heads(fh[rows, BLK:], rows)
    ld_k.wait()
    ld_v.wait()
    bias = stale_bias(first, length)
    next_first, next_length = patch_at(1)
    next_bias = stale_bias(next_first, next_length)

    def unit_rows(i):
        return pl.ds(mult(i * UNIT, UNIT), UNIT)

    def unit1_rows(i):
        return pl.ds(mult(i * UNIT1, UNIT1), UNIT1)

    def att1_copy(i):
        part = att1.at[pl.ds(mult(i * CHUNK, CHUNK), CHUNK), own_cols]
        return remote(part, part, a1_s.at[i], a1_r.at[i], s, mate)

    def p1_copy(i, v):
        rows = unit1_rows(i)
        return remote(sb1.at[v, rows], rb1.at[v, rows], p1_s.at[v, i], p1_r.at[v, i], pair, slab[v])

    def f1_copy(i):
        rows = unit1_rows(i)
        return remote(fw1.at[rows], xs.at[rows], f1_s.at[i], f1_r.at[i], ahead, q)

    for copy in ld_res:
        copy.wait()
    for copy in res_copies:
        copy.wait_recv()
    for copy in ld_w[:4]:
        copy.wait()
    for copy in w_copies[:4]:
        copy.wait_recv()

    gate1 = [gates(slab[0]), gates(slab[1])]

    def s2_copy(g, k):
        return remote(st2.at[0, g], st2.at[k, g], s2_s.at[k - 1, g], s2_r.at[k - 1, g], s, peer[k])

    def rx_copy(g):
        v = jnp.where(g // 2 == j, 0, 1)
        src = xs.at[pl.ds(mult(g * ROWS, ROWS), ROWS)]
        return remote(src, rx.at[v], rx_s.at[v], rx_r.at[v], s, mate)

    def ready(g):
        hf = xs[pl.ds(mult(g * ROWS, ROWS), ROWS), :].astype(F32)
        mean = jnp.sum(hf, axis=1, keepdims=True) * (1.0 / SLAB)
        cent = hf - mean
        spread = jnp.sum(cent * cent, axis=1, keepdims=True)
        tile = jnp.where(lane == sub, mean, jnp.where(lane == sub + ROWS, spread, 0.0))
        st2[0, g] = jnp.sum(tile, axis=0, keepdims=True)
        for k in (2, 3, 1):
            s2_copy(g, k).start()

        @pl.when(g % 2 != c)
        def _():
            rx_copy(g).start()

    def process(g):
        for k in (1, 2, 3):
            s2_copy(g, k).wait_recv()
        stats = [st2[k, g] for k in range(4)]
        total = stats[0] + stats[1] + stats[2] + stats[3]
        means = total * 0.25
        apart = jnp.zeros((1, 128), F32)
        for stat in stats:
            apart = apart + (stat - means) * (stat - means) * SLAB
        both = jnp.where(lane[:1] < ROWS, apart, total)
        mean = jnp.sum(jnp.where(lane == sub, means, 0.0), axis=1, keepdims=True)
        spread = jnp.sum(
            jnp.where((lane == sub) | (lane == sub + ROWS), both, 0.0), axis=1, keepdims=True
        )
        rstd = lax.rsqrt(spread * (1.0 / WIDTH) + EPS)
        rows = pl.ds(mult(g * ROWS, ROWS), ROWS)
        modded = ((xs[rows, :BLK].astype(F32) - mean) * rstd * scale_h + shift_h).astype(BF16)
        fh[rows, BLK:] = modded
        heads(modded, rows)

        @pl.when(g < groups - 1)
        def _():
            attend_stale(rows, next_bias)

    def take(g):
        for u in range(ROWS // UNIT1):
            i = g * (ROWS // UNIT1) + u
            for v in (0, 1):
                p1_copy(i, v).wait_recv()
            rows = unit1_rows(i)
            held = (rb1[0, rows, :].astype(F32) + rb1[1, rows, :].astype(F32)).astype(BF16)

            @pl.when(even)
            def _():
                fw1[rows, :] = held
                f1_copy(i).start()

            @pl.when(jnp.logical_not(even))
            def _():
                xs[rows, :] = held

    def taken(g):
        for u in range(ROWS // UNIT1):
            f1_copy(g * (ROWS // UNIT1) + u).wait_recv()

    groups = PATCH // ROWS

    def step0(i, carry):
        rows = pl.ds(mult(i * CHUNK, CHUNK), CHUNK)
        live = lax.broadcasted_iota(jnp.int32, (CHUNK, HD), 0) + i * CHUNK < length
        att1[rows, own_cols] = attend(qb[rows, :], live, bias, length)
        att1_copy(i).start()
        att1_copy(i).wait_recv()
        live = lax.broadcasted_iota(jnp.int32, (CHUNK, SLAB), 0) + i * CHUNK < length
        keep = live & (i == j)
        for v in (0, 1):
            proj = jnp.dot(att1[rows, :], w4[slab[v]], preferred_element_type=F32)
            held = res[v].astype(F32)
            sb1[v, rows, :] = (proj * gate1[v] + jnp.where(keep, held, 0.0)).astype(BF16)
            for u in range(CHUNK // UNIT1):

                @pl.when(i * (CHUNK // UNIT1) + u < AT_ONCE)
                def _():
                    p1_copy(i * (CHUNK // UNIT1) + u, v).start()

        return carry

    lax.fori_loop(0, PATCH // CHUNK, step0, 0)

    def hand_over(i, carry):
        @pl.when(i < groups)
        def _():
            take(i)

        @pl.when((i < groups) & jnp.logical_not(even))
        def _():
            ready(i)

        @pl.when((i >= 1) & (i < 1 + groups) & even)
        def _():
            taken(i - 1)
            ready(i - 1)

        for u in range(AT_ONCE, UNITS1):

            @pl.when(i == (u - AT_ONCE) // 2)
            def _():
                for v in (0, 1):
                    p1_copy(u, v).start()

        @pl.when(i == 0)
        def _():
            refresh(first, length)

        done = i - 1 - (1 - odd)

        @pl.when((done >= 0) & (done < groups))
        def _():
            process(done)

        return carry

    lax.fori_loop(0, groups + 2, hand_over, 0)

    first, length = next_first, next_length

    def att2_copy(i):
        rows = pl.ds(mult(i * ROWS, ROWS), ROWS)
        return remote(as2.at[rows], att2.at[rows, own_cols], a2_s.at[i], a2_r.at[i], s, mate)

    def slab_of(u):
        p = u % 4
        return 2 * (p // 2) + (c + p % 2) % 2

    def p2_copy(u, e, v):
        return remote(sb2.at[v, u, e], rb2.at[v, u, e], p2_s.at[v, u, e], p2_r.at[v, u, e], pair, slab[v])

    def f2_copy(u, e):
        dst = out_ref.at[unit_rows(u // 4), block_cols(slab_of(u), e)]
        return remote(fw2.at[u, e], dst, f2_s.at[u, e], f2_r.at[u, e], ahead, q)

    for v in (0, 1):
        rx_copy(mate_slab[v]).wait_recv()
    for copy in ld_w[4:]:
        copy.wait()
    for copy in w_copies[4:]:
        copy.wait_recv()

    bases = [ROWS * slab[0], ROWS * slab[1], ROWS * mate_slab[0], ROWS * mate_slab[1]]

    def finish(u):
        for e in (0, 1):
            for v in (0, 1):
                p2_copy(u, e, v).wait_recv()
            held = (rb2[0, u, e].astype(F32) + rb2[1, u, e].astype(F32)).astype(BF16)

            @pl.when(even)
            def _():
                fw2[u, e] = held
                f2_copy(u, e).start()

            @pl.when(jnp.logical_not(even))
            def _():
                out_ref[unit_rows(u // 4), block_cols(slab_of(u), e)] = held

    r = lax.broadcasted_iota(jnp.int32, (4 * UNIT, HD), 0)
    seg = r // UNIT
    start = jnp.where(
        seg == 0, bases[0], jnp.where(seg == 1, bases[1], jnp.where(seg == 2, bases[2], bases[3]))
    )

    def merge(i, last=None):
        seen = [pl.ds(mult(base + UNIT * i, UNIT), UNIT) for base in bases]
        queries = jnp.concatenate([qb[part, :] for part in seen], axis=0)
        new = [fresh_scores(queries, h, length) for h in heads_here]
        if last is None:
            fresh = soften(new, fresh_values)
        else:
            late = qb[last, :]
            old = [stale_scores(late, h, next_bias) for h in heads_here]
            old_top, new_top = tops(old), tops(new)
            old = [weigh(part, m) for part, m in zip(old, old_top)]
            new = [weigh(part, m) for part, m in zip(new, new_top)]
            old_out = [stale_values(old[h][0], h) for h in heads_here]
            fresh = new_top, [part[1] for part in new], [fresh_values(new[h][0], h) for h in heads_here]
            keep_stale(last, old_top, [part[1] for part in old], old_out)
        out = jnp.concatenate([om[part, :] for part in seen], axis=0)
        tile = jnp.concatenate([ml[part, :] for part in seen], axis=0)
        live = start + UNIT * i + r % UNIT < length
        got = merge_parts(out, tile, fresh, live)
        rows = pl.ds(i * ROWS, ROWS)
        att2[rows, own_cols] = got[:ROWS]
        as2[rows, :] = got[ROWS:]
        att2_copy(i).start()

    merge(0, pl.ds(PATCH - ROWS, ROWS))
    merge(1)

    def step1(u, carry):
        n = u // 4
        p = u % 4

        @pl.when(p == 0)
        def _():
            att2_copy(n).wait_recv()

        g = slab_of(u)
        part = unit_rows(n)
        left = att2[pl.ds(mult(n * ROWS, ROWS), ROWS), :]
        proj = jnp.dot(left, w4[g], preferred_element_type=F32) * gates(g)
        own = jnp.concatenate(
            [xs[pl.ds(mult(base + UNIT * n, UNIT), UNIT), :] for base in bases[:2]], axis=0
        )
        his = jnp.concatenate([rx[0, part, :], rx[1, part, :]], axis=0)
        held = jnp.where(p % 2 == 0, own.astype(F32), his.astype(F32))
        proj = (proj + jnp.where(p // 2 == j, held, 0.0)).astype(BF16)
        for v in (0, 1):
            for e in (0, 1):
                sb2[v, u, e] = proj[v * UNIT : (v + 1) * UNIT, e * BLK : (e + 1) * BLK]
                p2_copy(u, e, v).start()

        @pl.when(even)
        def _():
            finish(u)

        return carry

    lax.fori_loop(0, UNITS, step1, 0)

    @pl.when(jnp.logical_not(even))
    def _():
        def rest(u, carry):
            finish(u)
            return carry

        lax.fori_loop(0, UNITS, rest, 0)

    @pl.when(even)
    def _():
        for i in range(UNITS1):
            f1_copy(i).wait_send()
        for u in range(UNITS):
            for e in (0, 1):
                f2_copy(u, e).wait()

    for k in (1, 2, 3):
        md_copies[k].wait_send()
        for g in range(groups):
            s2_copy(g, k).wait_send()
    for v in (0, 1):
        rx_copy(mate_slab[v]).wait_send()
    for copy in res_copies + w_copies:
        copy.wait_send()
    for i in range(PATCH // CHUNK):
        att1_copy(i).wait_send()
    for i in range(UNITS1):
        for v in (0, 1):
            p1_copy(i, v).wait_send()
    for u in range(UNITS):
        for v in (0, 1):
            for e in (0, 1):
                p2_copy(u, e, v).wait_send()
    for i in range(2):
        att2_copy(i).wait_send()


def shards(n_pipe, *args):
    dma = pltpu.SemaphoreType.DMA
    vmem = pltpu.VMEM
    any_space = pl.BlockSpec(memory_space=pl.ANY)
    smem = pl.BlockSpec(memory_space=pltpu.SMEM)
    chunks = PATCH // ROWS
    held = [pltpu.with_memory_space_constraint(arg, pltpu.HBM) for arg in args[:10]]
    return pl.pallas_call(
        functools.partial(kernel, n_pipe),
        out_shape=jax.ShapeDtypeStruct((ROWS, WIDTH), BF16),
        in_specs=[any_space] * 10 + [smem],
        out_specs=pl.BlockSpec(memory_space=vmem),
        scratch_shapes=[
            vmem((ROWS, WIDTH), BF16),
            vmem((CAP, BLK), BF16),
            vmem((CAP, BLK), BF16),
            vmem((4, SLAB, SLAB), BF16),
            vmem((1, WIDTH), F32),
            vmem((1, WIDTH), F32),
            vmem((1, WIDTH), F32),
            vmem((1, HD), F32),
            vmem((1, HD), F32),
            vmem((ROWS, HALF), BF16),
            vmem((2, 2 * ROWS, SLAB), BF16),
            vmem((PATCH, BLK), BF16),
            vmem((PATCH, SLAB), BF16),
            vmem((PATCH, SLAB), BF16),
            vmem((2, PATCH, SLAB), BF16),
            vmem((2, PATCH, SLAB), BF16),
            vmem((PATCH, SLAB), BF16),
            vmem((PATCH, SLAB), BF16),
            vmem((4, chunks, 1, 128), F32),
            vmem((PATCH, BLK), F32),
            vmem((PATCH, 128), F32),
            vmem((2, ROWS, SLAB), BF16),
            vmem((2 * ROWS, BLK), BF16),
            vmem((2 * ROWS, SLAB), BF16),
            vmem((2, UNITS, 2, UNIT, BLK), BF16),
            vmem((2, UNITS, 2, UNIT, BLK), BF16),
            vmem((UNITS, 2, UNIT, BLK), BF16),
            pltpu.SMEM((NP,), jnp.int32),
            dma((21,)),
            dma((3,)),
            dma((3,)),
            dma((4,)),
            dma((4,)),
            dma((8,)),
            dma((8,)),
            dma((PATCH // CHUNK,)),
            dma((PATCH // CHUNK,)),
            dma((2, UNITS1)),
            dma((2, UNITS1)),
            dma((UNITS1,)),
            dma((UNITS1,)),
            dma((3, chunks)),
            dma((3, chunks)),
            dma((2,)),
            dma((2,)),
            dma((2,)),
            dma((2,)),
            dma((2, UNITS, 2)),
            dma((2, UNITS, 2)),
            dma((UNITS, 2)),
            dma((UNITS, 2)),
        ],
        compiler_params=pltpu.CompilerParams(
            collective_id=0, has_side_effects=True, vmem_limit_bytes=40 << 20
        ),
        name="section_steps",
    )(*held, args[10])


def solution(mesh):
    in_specs = (
        P(("pipe", "seq"), None),
        P("pipe", None, "seq"),
        P("pipe", None, "seq"),
        P("pipe", "seq", None),
        P("pipe", None),
        P("pipe", None),
        P("pipe", None),
        P("pipe", None),
        P("pipe", None),
        P(),
        P(),
    )
    return jax.shard_map(
        functools.partial(shards, mesh.shape["pipe"]),
        mesh=mesh,
        in_specs=in_specs,
        out_specs=P(("pipe", "seq"), None),
        check_vma=False,
    )
```
